512 devices in a mesh: stream: 32 (over y, z_lo), span: 16 (over x, z_hi, core).
Axes of the slice: x: 4, y: 8, z: 8 (z_hi: 2, z_lo: 4; z = z_hi * 4 + z_lo), core: 2. Of those that a mesh axis runs over, the one named last changes fastest.
Arguments:
- right_sides: bfloat16 [32, 16, 4, 512, 128], P('stream', 'span'), may hold values from -2.5 to 2.5
- inverse: bfloat16 [32, 16, 4, 512, 512], P('stream', 'span'), as said below
- coupling: bfloat16 [32, 16, 4, 3, 64, 512], P('stream', 'span')
- sweep_order: int32 [32, 16, 4], P('stream', 'span'), may hold values from 0 to 3, each once within a row
Outputs:
- solution: bfloat16 [32, 16, 4, 512, 128], P('stream', 'span')
The draws below stay inside these ranges and needn't reach their ends.
Inputs may be any that keep to these rules, and one draw needn't show every extreme that they name: `sweep_order`: each group's 4 slots appear once each. Every diagonal block's inverse is well conditioned and of order one.
All inputs are finite; a program needn't handle non-finite values.
Results may differ from the reference program's by a relative error of at most 0.024.
Values may be sent and summed in bfloat16 or wider, within the bound.
A program may use at most 64 MiB of HBM per device.

```python
import jax
import jax.numpy as jnp
from jax import lax

NP = 8
NODES = 512
FACE = 64
EL = 4
RHS = 128
SWEEPS = 6
SGROUPS = 32
PGROUPS = 16


def draw_inverse(key, part):
    shape = (SGROUPS, PGROUPS, EL, NODES, NODES)
    key_diag, key_off = jax.random.split(jax.random.fold_in(key, 11))
    off_part = jax.random.normal(key_off, shape, jnp.float32) * (0.5 / NODES ** 0.5)
    diag_part = jax.random.uniform(key_diag, shape[:-1], jnp.float32, 0.6, 1.4)
    row_ids = jnp.arange(NODES, dtype=jnp.int32)[:, None]
    col_ids = jnp.arange(NODES, dtype=jnp.int32)[None, :]
    carried = jnp.logical_and(col_ids < FACE, row_ids == col_ids + (NP - 1) * FACE).astype(jnp.float32)
    return (off_part + diag_part[..., None] * jnp.eye(NODES, dtype=jnp.float32) + carried).astype(jnp.bfloat16)


def draw_coupling(key, part):
    shape = (SGROUPS, PGROUPS, EL, 3, FACE, NODES)
    scales = jnp.array([0.096 / FACE ** 0.5, 0.15 / FACE ** 0.5, 0.15 / FACE ** 0.5], jnp.float32)[:, None, None]
    base_key = jax.random.fold_in(key, 23)
    key_noise, key_main = jax.random.split(base_key)
    values = jax.random.normal(key_noise, shape, jnp.float32)
    centre = (0.961 / (1.0 + 0.25 / NP)) ** 0.5
    main_part = jax.random.uniform(key_main, (SGROUPS, PGROUPS, EL, FACE), jnp.float32, centre - 0.03, centre + 0.03)
    face_ids = jnp.arange(FACE, dtype=jnp.int32)[:, None]
    node_ids = jnp.arange(NODES, dtype=jnp.int32)[None, :]
    matching = (face_ids == node_ids).astype(jnp.float32)
    first_only = (jnp.arange(3, dtype=jnp.int32) == 0).astype(jnp.float32)[:, None, None]
    placed = main_part[:, :, :, None, :, None] * (first_only * matching)[None, None, None]
    return (values * scales + placed).astype(jnp.bfloat16)


def block_scale(own_key, dims, cuts, smallest, high):
    def one(dim, blocks):
        steps = jax.random.uniform(jax.random.fold_in(jax.random.fold_in(own_key, 6), dim), (blocks,), jnp.float32, smallest / len(cuts), high / len(cuts))
        return jnp.repeat(jnp.exp(steps), dims[dim] // blocks).reshape((-1,) + (1,) * (len(dims) - dim - 1))

    gain = one(*cuts[0])
    for cut in cuts[1:]:
        gain = gain * one(*cut)
    return gain


def scatter_about(own_key, dims, spread, bound, cuts=(), held_as=jnp.bfloat16):
    factor_of = block_scale(own_key, dims, cuts, -0.22, 0.18) if cuts else 1.0
    values = jax.random.normal(own_key, dims, jnp.float32) * spread * factor_of
    return jnp.minimum(jnp.maximum(values, -bound), bound).astype(held_as)


def setup_inputs(seed: int = 0) -> dict:
    keys = jax.random.split(jax.random.key(seed), 5)
    right_sides = scatter_about(keys[0], (SGROUPS, PGROUPS, EL, NODES, RHS), 0.4, 2.5, ((0, 32), (1, 16)))
    inverse = draw_inverse(jax.random.fold_in(keys[4], 71), 0)
    coupling = draw_coupling(jax.random.fold_in(keys[4], 71), 0)
    sweep_order = jax.vmap(lambda own: jax.random.permutation(own, EL))(jax.random.split(keys[3], SGROUPS * PGROUPS)).reshape((SGROUPS, PGROUPS, EL)).astype(jnp.int32)
    return {"right_sides": right_sides, "inverse": inverse, "coupling": coupling, "sweep_order": sweep_order}


def face_rows(values, layer):
    leading = values.shape[:-2]
    columns = values.shape[-1]
    shaped = values.reshape(leading + (NP, NP, NP, columns))
    return shaped[..., :, layer, :, :].reshape(leading + (NP * NP, columns))


def select_slots(values, chosen):
    return jax.vmap(lambda blocks, picks: blocks[picks])(values, chosen)


def reference(right_sides, inverse, coupling, sweep_order):
    highest = lax.Precision.HIGHEST

    def lifting_group(items):
        inverse_group, coupling_group, order_group = items
        inverse_pos = select_slots(inverse_group, order_group).astype(jnp.float32)
        inflow_pos = select_slots(coupling_group, order_group)[:, :, 0].astype(jnp.float32)
        return jnp.einsum("penm,pefm->penf", inverse_pos, inflow_pos, precision=highest)

    liftings = lax.map(lifting_group, (inverse, coupling, sweep_order))
    solution = jnp.zeros(right_sides.shape, jnp.bfloat16)
    for sweep_index in range(SWEEPS):
        upper_layer = face_rows(solution, NP - 1)
        lower_layer = face_rows(solution, 0)
        blank = jnp.zeros_like(upper_layer[:, :1])
        from_below = jnp.concatenate([blank, upper_layer[:, :-1]], axis=1)
        from_above = jnp.concatenate([lower_layer[:, 1:], blank], axis=1)

        def group_step(inflow, items):
            inverse_group, coupling_group, rhs_group, order_group, below, above, lifting = items
            inverse_pos = select_slots(inverse_group, order_group).astype(jnp.float32)
            coupling_pos = select_slots(coupling_group, order_group).astype(jnp.float32)
            rhs_pos = select_slots(rhs_group, order_group).astype(jnp.float32)
            source = rhs_pos + jnp.einsum("pefn,pefr->penr", coupling_pos[:, :, 1], below.astype(jnp.float32), precision=highest)
            source = source + jnp.einsum("pefn,pefr->penr", coupling_pos[:, :, 2], above.astype(jnp.float32), precision=highest)
            source = source.astype(jnp.bfloat16)
            gained = jnp.einsum("penm,pemr->penr", inverse_pos, source.astype(jnp.float32), precision=highest)
            pieces = []
            for position in range(EL):
                added = jnp.einsum("pnf,pfr->pnr", lifting[:, position], inflow, precision=highest)
                pieces.append((gained[:, position] + added).astype(jnp.bfloat16))
                inflow = jnp.einsum("pgf,pfr->pgr", lifting[:, position, NODES - FACE:], inflow, precision=highest) + gained[:, position, NODES - FACE:]
            return inflow, jnp.stack(pieces, axis=1)

        start = jnp.zeros((PGROUPS, FACE, RHS), jnp.float32)
        final_trace, solution = lax.scan(group_step, start, (inverse, coupling, right_sides, sweep_order, from_below, from_above, liftings))
    placed = jax.vmap(jax.vmap(lambda blocks, picks: jnp.zeros_like(blocks).at[picks].set(blocks)))(solution, sweep_order)
    return placed
```

```python
import jax
import jax.numpy as jnp
from jax import lax
from jax.experimental import pallas as pl
from jax.experimental.pallas import tpu as pltpu
from jax.sharding import PartitionSpec as P

SWEEPS = 6
EL = 4
NODES = 512
FACE = 64
RHS = 128
ROW = 4
F32 = jnp.float32
BF16 = jnp.bfloat16
MESH = pl.DeviceIdType.MESH


def mm(left, right):
    return jnp.dot(left, right, preferred_element_type=F32)


def mm_nt(left, right):
    return lax.dot_general(left, right, (((1,), (1,)), ((), ())), preferred_element_type=F32)


def split(value):
    high = value.astype(BF16)
    return high, (value - high.astype(F32)).astype(BF16)


def left_pair(value):
    return jnp.concatenate(split(value), axis=1)


def twice(value):
    return jnp.concatenate([value, value], axis=0)


def mm_fine(pair, right):
    high, low = split(right)
    return mm(
        jnp.concatenate([pair, pair[:, :FACE]], axis=1),
        jnp.concatenate([high, high, low], axis=0),
    )


def faces_of(values):
    lower = [values[64 * a : 64 * a + 8] for a in range(8)]
    upper = [values[64 * a + 56 : 64 * a + 64] for a in range(8)]
    return jnp.concatenate([values[NODES - FACE :]] + lower + upper, axis=0)


def kernel(
    rows, spans,
    order_ref, rs_hbm, inv_hbm, cpl_hbm,
    out_hbm,
    rs, inv, cpl, out_v,
    lift_full, side_full, gain_full, lift_face, side_face, gain_face,
    o_mat, f_mat, fe_mat, o_const, f_const, s_mat, se_mat, s_const,
    step_mats, inflow,
    xbuf, ysend, offbuf, tbuf, cin, csend, pre, pre_out,
    in_sem, out_sem, row_s, row_r, t_s, t_r, c_s, c_r, face_s, face_r,
):
    g = lax.axis_index("stream")
    s = lax.axis_index("span")
    y = g // ROW
    z = g % ROW

    def in_copies(t):
        return [
            pltpu.make_async_copy(inv_hbm.at[t], inv.at[t], in_sem.at[t, 0]),
            pltpu.make_async_copy(cpl_hbm.at[t], cpl.at[t], in_sem.at[t, 1]),
            pltpu.make_async_copy(rs_hbm.at[t], rs.at[t], in_sem.at[t, 2]),
        ]

    for t in range(EL):
        for c in in_copies(t):
            c.start()

    has_up = y > 0
    has_down = y < rows - 1
    has_below = s > 0
    has_above = s < spans - 1

    barrier = pltpu.get_barrier_semaphore()

    def greet(a, b):
        pl.semaphore_signal(barrier, inc=1, device_id=(a, b), device_id_type=MESH)

    for j in range(1, ROW):
        greet(y * ROW + (z + j) % ROW, s)
    pl.when(has_up)(lambda: greet(g - ROW, s))
    pl.when(has_down)(lambda: greet(g + ROW, s))
    pl.when(has_below)(lambda: greet(g, s - 1))
    pl.when(has_above)(lambda: greet(g, s + 1))

    xbuf[0] = jnp.zeros((2, EL, FACE, RHS), BF16)

    @pl.when(jnp.logical_not(has_below))
    def _():
        for k in range(1, SWEEPS):
            xbuf[k, 0] = jnp.zeros((EL, FACE, RHS), BF16)

    @pl.when(jnp.logical_not(has_above))
    def _():
        for k in range(1, SWEEPS):
            xbuf[k, 1] = jnp.zeros((EL, FACE, RHS), BF16)

    @pl.when(jnp.logical_not(has_up))
    def _():
        cin[...] = jnp.zeros(cin.shape, BF16)

    for t in range(EL):
        for c in in_copies(t):
            c.wait()
        maps = mm_nt(inv[t], cpl[t])
        gains = mm(inv[t], rs[t])
        lift_full[t] = left_pair(maps[:, :FACE])
        side_full[t] = maps[:, FACE:].astype(BF16)
        gain_full[t] = gains
        chosen = faces_of(maps)
        lift_face[t] = left_pair(chosen[:, :FACE])
        side_face[t] = chosen[:, FACE:]
        gain_face[t] = faces_of(gains)

    slots = [order_ref[p] for p in range(EL)]
    blocks = None
    f_mat[...] = jnp.zeros(f_mat.shape, BF16)
    s_mat[...] = jnp.zeros(s_mat.shape, BF16)
    for p in range(EL):
        lift = lift_face[slots[p]]
        side = side_face[slots[p]]
        gain = gain_face[slots[p]]
        if p == 0:
            lift_own = lift[:, :FACE].astype(F32) + lift[:, FACE:].astype(F32)
            result = jnp.concatenate([side, gain, lift_own], axis=1)
        else:
            moved = mm_fine(lift, blocks)
            result = jnp.concatenate(
                [moved[:, : 128 * p], side, moved[:, 128 * p : 128 * p + 128] + gain, moved[:, 128 * p + 128 :]],
                axis=1,
            )
        wide = 128 * (p + 1)
        for layer in range(2):
            at = layer * EL * FACE + p * FACE
            part = result[FACE + layer * FACE : 2 * FACE + layer * FACE]
            f_mat[at : at + FACE, :wide] = part[:, :wide].astype(BF16)
            f_const[at : at + FACE] = part[:, wide : wide + 128]
            fe_mat[at : at + FACE] = left_pair(part[:, wide + 128 :])
        blocks = result[:FACE]
        if p < EL - 1:
            s_mat[p * FACE : p * FACE + FACE, :wide] = blocks[:, :wide].astype(BF16)
            s_const[p * FACE : p * FACE + FACE] = blocks[:, wide : wide + 128]
            se_mat[p * FACE : p * FACE + FACE] = left_pair(blocks[:, wide + 128 :])
    o_mat[...] = blocks[:, :512].astype(BF16)
    o_const[...] = blocks[:, 512:640]
    tbuf[z] = left_pair(blocks[:, 640:])
    offbuf[0, z] = blocks[:, 512:640].astype(BF16)

    greetings = (
        ROW - 1
        + has_up.astype(jnp.int32)
        + has_down.astype(jnp.int32)
        + has_below.astype(jnp.int32)
        + has_above.astype(jnp.int32)
    )
    pl.semaphore_wait(barrier, greetings)

    def map_copy(j, who):
        return pltpu.make_async_remote_copy(
            tbuf.at[who], tbuf.at[who], t_s.at[j - 1], t_r.at[j - 1],
            device_id=(y * ROW + (z + j) % ROW, s), device_id_type=MESH,
        )

    def row_copy(k, j, who):
        return pltpu.make_async_remote_copy(
            offbuf.at[k, who], offbuf.at[k, who], row_s.at[k, j - 1], row_r.at[k, j - 1],
            device_id=(y * ROW + (z + j) % ROW, s), device_id_type=MESH,
        )

    def carry_copy(k):
        return pltpu.make_async_remote_copy(
            csend.at[k], cin.at[k], c_s.at[k], c_r.at[k],
            device_id=(g + ROW, s), device_id_type=MESH,
        )

    def face_copy(k, layer):
        return pltpu.make_async_remote_copy(
            ysend.at[k, layer], xbuf.at[k + 1, 1 - layer], face_s.at[k, layer], face_r.at[k, layer],
            device_id=(g, s - 1 if layer == 0 else s + 1), device_id_type=MESH,
        )

    def stacked(k):
        return jnp.concatenate(
            [xbuf[k, side, p] for p in range(EL) for side in range(2)], axis=0
        )

    for j in range(1, ROW):
        map_copy(j, z).start()
    for j in range(1, ROW):
        row_copy(0, j, z).start()

    for j in range(1, ROW):
        map_copy(j, (z + ROW - j) % ROW).wait_recv()
    state = None
    eye = (
        lax.broadcasted_iota(jnp.int32, (FACE, FACE), 0) == lax.broadcasted_iota(jnp.int32, (FACE, FACE), 1)
    ).astype(F32)
    none = jnp.zeros((FACE, FACE), F32)
    state = jnp.concatenate([none] * ROW + [eye], axis=1)
    for q in range(ROW + 1):
        step_mats[q] = jnp.concatenate(
            [left_pair(state[:, : ROW * FACE]), left_pair(state[:, ROW * FACE :])], axis=1
        )
        if q < ROW:
            state = mm_fine(tbuf[q], state) + jnp.concatenate(
                [eye if r == q else none for r in range(ROW)] + [none], axis=1
            )

    def row_stage(k):
        for j in range(1, ROW):
            row_copy(k, j, (z + ROW - j) % ROW).wait_recv()
        offsets = jnp.concatenate([offbuf[k, q] for q in range(ROW)], axis=0)
        both = jnp.concatenate([step_mats[ROW], step_mats[z]], axis=0)
        local = mm(both[:, : 2 * ROW * FACE], twice(offsets))

        @pl.when(has_up)
        def _():
            carry_copy(k).wait_recv()

        full = local + mm(both[:, 2 * ROW * FACE :], twice(cin[k]))

        @pl.when(has_down)
        def _():
            csend[k] = full[:FACE].astype(BF16)
            carry_copy(k).start()

        return full[FACE:].astype(BF16)

    @pl.loop(0, SWEEPS - 1)
    def _(k):
        pre[...] = mm(f_mat[...], stacked(k)) + f_const[...]
        entry = row_stage(k)
        faces = (pre[...] + mm(fe_mat[...], twice(entry))).astype(BF16)
        for layer in range(2):
            for p in range(EL):
                at = layer * EL * FACE + p * FACE
                ysend[k, layer, p] = faces[at : at + FACE]

        @pl.when(has_below)
        def _():
            face_copy(k, 0).start()

        @pl.when(has_above)
        def _():
            face_copy(k, 1).start()

        @pl.when(has_above)
        def _():
            face_copy(k, 0).wait_recv()

        @pl.when(has_below)
        def _():
            face_copy(k, 1).wait_recv()

        offbuf[k + 1, z] = (mm(o_mat[...], stacked(k + 1)) + o_const[...]).astype(BF16)
        for j in range(1, ROW):
            row_copy(k + 1, j, z).start()

    last = SWEEPS - 1
    places = []
    for t in range(EL):
        place = jnp.int32(0)
        for p in range(1, EL):
            place = jnp.where(slots[p] == t, p, place)
        places.append(place)
    traces = mm(s_mat[...], stacked(last)) + s_const[...]
    for t in range(EL):
        sides = jnp.concatenate([xbuf[last, 0, places[t]], xbuf[last, 1, places[t]]], axis=0)
        pre_out[t] = gain_full[t] + mm(side_full[t], sides)
    entry = row_stage(last)
    traces = (traces + mm(se_mat[...], twice(entry))).astype(BF16)
    inflow[0] = entry
    for p in range(1, EL):
        inflow[p] = traces[(p - 1) * FACE : p * FACE]

    def out_copy(t):
        return pltpu.make_async_copy(out_v.at[t], out_hbm.at[t], out_sem.at[t])

    for t in range(EL):
        out_v[t] = (pre_out[t] + mm(lift_full[t], twice(inflow[places[t]]))).astype(BF16)
        out_copy(t).start()

    for j in range(1, ROW):
        map_copy(j, z).wait_send()

    @pl.loop(0, SWEEPS)
    def _(k):
        for j in range(1, ROW):
            row_copy(k, j, z).wait_send()
        pl.when(has_down)(lambda: carry_copy(k).wait_send())

    @pl.loop(0, SWEEPS - 1)
    def _(k):
        pl.when(has_below)(lambda: face_copy(k, 0).wait_send())
        pl.when(has_above)(lambda: face_copy(k, 1).wait_send())

    for t in range(EL):
        out_copy(t).wait()


def shards(rows, spans, right_sides, inverse, coupling, sweep_order):
    vmem = pltpu.VMEM
    dma = pltpu.SemaphoreType.DMA
    any_space = pl.BlockSpec(memory_space=pltpu.HBM)
    placed = pl.pallas_call(
        lambda *refs: kernel(rows, spans, *refs),
        name="sweeps",
        out_shape=jax.ShapeDtypeStruct((EL, NODES, RHS), BF16),
        in_specs=[pl.BlockSpec(memory_space=pltpu.SMEM), any_space, any_space, any_space],
        out_specs=any_space,
        scratch_shapes=[
            vmem((EL, NODES, RHS), BF16),
            vmem((EL, NODES, NODES), BF16),
            vmem((EL, 3 * FACE, NODES), BF16),
            vmem((EL, NODES, RHS), BF16),
            vmem((EL, NODES, 2 * FACE), BF16),
            vmem((EL, NODES, 2 * FACE), BF16),
            vmem((EL, NODES, RHS), F32),
            vmem((EL, 3 * FACE, 2 * FACE), BF16),
            vmem((EL, 3 * FACE, 2 * FACE), F32),
            vmem((EL, 3 * FACE, RHS), F32),
            vmem((FACE, 512), BF16),
            vmem((512, 512), BF16),
            vmem((512, 2 * FACE), BF16),
            vmem((FACE, RHS), F32),
            vmem((512, RHS), F32),
            vmem((3 * FACE, 512), BF16),
            vmem((3 * FACE, 2 * FACE), BF16),
            vmem((3 * FACE, RHS), F32),
            vmem((ROW + 1, FACE, 2 * (ROW * FACE + FACE)), BF16),
            vmem((EL, FACE, RHS), BF16),
            vmem((SWEEPS, 2, EL, FACE, RHS), BF16),
            vmem((SWEEPS - 1, 2, EL, FACE, RHS), BF16),
            vmem((SWEEPS, ROW, FACE, RHS), BF16),
            vmem((ROW, FACE, 128), BF16),
            vmem((SWEEPS, FACE, RHS), BF16),
            vmem((SWEEPS, FACE, RHS), BF16),
            vmem((512, RHS), F32),
            vmem((EL, NODES, RHS), F32),
            dma((EL, 3)),
            dma((EL,)),
            dma((SWEEPS, ROW - 1)),
            dma((SWEEPS, ROW - 1)),
            dma((ROW - 1,)),
            dma((ROW - 1,)),
            dma((SWEEPS,)),
            dma((SWEEPS,)),
            dma((SWEEPS - 1, 2)),
            dma((SWEEPS - 1, 2)),
        ],
        compiler_params=pltpu.CompilerParams(
            collective_id=0, has_side_effects=True, vmem_limit_bytes=58 * 2**20
        ),
    )(
        sweep_order[0, 0],
        right_sides[0, 0],
        inverse[0, 0],
        coupling[0, 0].reshape(EL, 3 * FACE, NODES),
    )
    return placed[None, None]


def solution(mesh):
    rows = mesh.shape["stream"] // ROW
    spans = mesh.shape["span"]
    in_specs = (
        P("stream", "span", None, None, None),
        P("stream", "span", None, None, None),
        P("stream", "span", None, None, None, None),
        P("stream", "span", None),
    )
    out_specs = P("stream", "span", None, None, None)

    def run(right_sides, inverse, coupling, sweep_order):
        return shards(rows, spans, right_sides, inverse, coupling, sweep_order)

    return jax.shard_map(run, mesh=mesh, in_specs=in_specs, out_specs=out_specs, check_vma=False)
```

```python
import jax
import jax.numpy as jnp
from jax import lax
from jax.experimental import pallas as pl
from jax.experimental.pallas import tpu as pltpu
from jax.sharding import PartitionSpec as P

SWEEPS = 6
EL = 4
NODES = 512
FACE = 64
RHS = 128
NB = 4
F32 = jnp.float32
BF16 = jnp.bfloat16
MESH = pl.DeviceIdType.MESH


def mm(left, right):
    return jnp.dot(left, right, preferred_element_type=F32)


def mm_nt(left, right):
    return lax.dot_general(left, right, (((1,), (1,)), ((), ())), preferred_element_type=F32)


def split(value):
    high = value.astype(BF16)
    return high, (value - high.astype(F32)).astype(BF16)


def left_pair(value):
    return jnp.concatenate(split(value), axis=1)


def twice(value):
    return jnp.concatenate([value, value], axis=0)


def mm_fine(pair, right):
    high, low = split(right)
    return mm(
        jnp.concatenate([pair, pair[:, :FACE]], axis=1),
        jnp.concatenate([high, high, low], axis=0),
    )


def faces_of(values):
    lower = [values[64 * a : 64 * a + 8] for a in range(8)]
    upper = [values[64 * a + 56 : 64 * a + 64] for a in range(8)]
    return jnp.concatenate([values[NODES - FACE :]] + lower + upper, axis=0)


def kernel(
    blocks_along, spans,
    order_ref, rs_hbm, inv_hbm, cpl_hbm,
    out_hbm,
    rs, inv, cpl, out_v,
    lift_full, side_full, gain_full, lift_face, side_face, gain_face,
    pf_mat, pf_const, fe_next, s_mat, se_mat, s_const,
    m_all, d_all, local, inflow, xs, pre_out,
    hsend, hbuf, msend, asend, mbuf, abuf, xbuf, ysend, ebuf, obuf, esend, pbuf, psend, cin, csend, efin,
    in_sem, out_sem, h_s, h_r, m_s, m_r, a_s, a_r,
    face_s, face_r, e_s, e_r, o_s, o_r, p_s, p_r, c_s, c_r, fin_s, fin_r,
):
    g = lax.axis_index("stream")
    s = lax.axis_index("span")
    block = g // NB
    m = g % NB

    odd = s % 2

    def owner_of(column):
        return block * NB + (NB - 1) * (column % 2), column - column % 2 + 1

    first_place = (m == 0).astype(jnp.int32)
    is_owner = jnp.logical_and(odd == 1, jnp.logical_or(m == 0, m == NB - 1))
    owned = s - first_place * odd
    owns_other = jnp.logical_and(is_owner, owned != s)
    owns_own = jnp.logical_and(is_owner, owned == s)
    has_up = block > 0
    has_down = block < blocks_along - 1
    has_side = (s > 0, s < spans - 1)
    owned_side = (owned > 0, owned < spans - 1)
    shift = (-1, 1)
    side_owner = (owner_of(s + 15), owner_of(s + 17))
    side_owner = tuple((a, b - 16) for a, b in side_owner)
    near_owner = tuple((a, b - 16) for a, b in (owner_of(owned + 15), owner_of(owned + 17)))
    own_owner = owner_of(s)
    to_self = (owns_other, jnp.bool_(False))

    def in_copies(t):
        return [
            pltpu.make_async_copy(inv_hbm.at[t], inv.at[t], in_sem.at[t, 0]),
            pltpu.make_async_copy(cpl_hbm.at[t], cpl.at[t], in_sem.at[t, 1]),
            pltpu.make_async_copy(rs_hbm.at[t], rs.at[t], in_sem.at[t, 2]),
        ]

    for t in range(EL):
        for c in in_copies(t):
            c.start()

    barrier = pltpu.get_barrier_semaphore()

    def greet(a, b):
        pl.semaphore_signal(barrier, inc=1, device_id=(a, b), device_id_type=MESH)

    def both(a, b):
        return jnp.logical_and(a, b)

    not_owner = jnp.logical_not(is_owner)
    not_own = jnp.logical_not(owns_own)
    for side in range(2):
        @pl.when(has_side[side])
        def _():
            greet(g, s + shift[side])

            @pl.when(jnp.logical_not(to_self[side]))
            def _():
                greet(*side_owner[side])

        @pl.when(both(is_owner, owned_side[side]))
        def _():
            greet(*near_owner[side])
            for q in range(NB):
                @pl.when(jnp.logical_not(both(owned + shift[side] == s, m == q)))
                def _():
                    greet(block * NB + q, owned + shift[side])

        @pl.when(jnp.logical_not(has_side[side]))
        def _():
            hbuf[side] = jnp.zeros((256, 128), BF16)
            for k in range(SWEEPS - 1):
                xbuf[k, side] = jnp.zeros((EL, FACE, RHS), BF16)
                ebuf[k, side] = jnp.zeros((FACE, RHS), BF16)

        @pl.when(both(is_owner, jnp.logical_not(owned_side[side])))
        def _():
            for k in range(SWEEPS - 1):
                obuf[k, side] = jnp.zeros((NB, FACE, RHS), BF16)
                pbuf[k, side] = jnp.zeros((NB, FACE, RHS), BF16)

    @pl.when(is_owner)
    def _():
        for q in range(NB):
            pl.when(jnp.logical_not(both(owned == s, m == q)))(lambda: greet(block * NB + q, owned))
        pl.when(has_up)(lambda: greet(g - NB, s))
        pl.when(has_down)(lambda: greet(g + NB, s))

    pl.when(not_own)(lambda: greet(*own_owner))

    @pl.when(jnp.logical_not(has_up))
    def _():
        cin[...] = jnp.zeros(cin.shape, BF16)

    for t in range(EL):
        for c in in_copies(t):
            c.wait()
        maps = mm_nt(inv[t], cpl[t])
        gains = mm(inv[t], rs[t])
        lift_full[t] = left_pair(maps[:, :FACE])
        side_full[t] = maps[:, FACE:].astype(BF16)
        gain_full[t] = gains
        chosen = faces_of(maps)
        lift_face[t] = left_pair(chosen[:, :FACE])
        side_face[t] = chosen[:, FACE:]
        gain_face[t] = faces_of(gains)

    slots = [order_ref[p] for p in range(EL)]
    trace = None
    pf_mat[...] = jnp.zeros(pf_mat.shape, BF16)
    s_mat[...] = jnp.zeros(s_mat.shape, BF16)
    face_entry = [[None] * EL, [None] * EL]
    for p in range(EL):
        lift = lift_face[slots[p]]
        side = side_face[slots[p]]
        gain = gain_face[slots[p]]
        if p == 0:
            lift_own = lift[:, :FACE].astype(F32) + lift[:, FACE:].astype(F32)
            result = jnp.concatenate([side, gain, lift_own], axis=1)
        else:
            moved = mm_fine(lift, trace)
            result = jnp.concatenate(
                [moved[:, : 128 * p], side, moved[:, 128 * p : 128 * p + 128] + gain, moved[:, 128 * p + 128 :]],
                axis=1,
            )
        wide = 128 * (p + 1)
        for layer in range(2):
            at = 128 + layer * EL * FACE + p * FACE
            part = result[FACE + layer * FACE : 2 * FACE + layer * FACE]
            pf_mat[at : at + FACE, :wide] = part[:, :wide].astype(BF16)
            pf_const[at : at + FACE] = part[:, wide : wide + 128]
            face_entry[layer][p] = part[:, wide + 128 :].astype(BF16)
            ysend[0, layer, p] = part[:, wide : wide + 128].astype(BF16)
        trace = result[:FACE]
        if p < EL - 1:
            s_mat[p * FACE : p * FACE + FACE, :wide] = trace[:, :wide].astype(BF16)
            s_const[p * FACE : p * FACE + FACE] = trace[:, wide : wide + 128]
            se_mat[p * FACE : p * FACE + FACE] = left_pair(trace[:, wide + 128 :])
    own_o = [
        jnp.concatenate([trace[:, 128 * p + 64 * side : 128 * p + 64 * side + 64] for p in range(EL)], axis=1).astype(BF16)
        for side in range(2)
    ]
    for side in range(2):
        fe = face_entry[side]
        hsend[side, :64] = own_o[side][:, :128]
        hsend[side, 64:128] = own_o[side][:, 128:]
        hsend[side, 128:] = jnp.concatenate(
            [jnp.concatenate([fe[0], fe[1]], axis=0), jnp.concatenate([fe[2], fe[3]], axis=0)], axis=1
        )
    msend[:64] = left_pair(trace[:, 640:])
    msend[64:] = trace[:, 512:640].astype(BF16)

    @pl.when(owns_own)
    def _():
        mbuf[m] = msend[...]

    def number(flag):
        return flag.astype(jnp.int32)

    greetings = 2 * (number(has_side[0]) + number(has_side[1])) - number(owns_other) + number(not_own)
    greetings = greetings + number(is_owner) * (
        (NB + 1) * (number(owned_side[0]) + number(owned_side[1]))
        + NB + number(has_up) + number(has_down)
    ) - number(owns_other) - number(owns_own)
    pl.semaphore_wait(barrier, greetings)

    def remote(src, dst, send, recv, a, b):
        return pltpu.make_async_remote_copy(src, dst, send, recv, device_id=(a, b), device_id_type=MESH)

    def h_copy(side):
        return remote(hsend.at[side], hbuf.at[1 - side], h_s.at[side], h_r.at[1 - side], g, s + shift[side])

    def h_arrival(side):
        return remote(hsend.at[side], hbuf.at[side], h_s.at[side], h_r.at[side], g, s + shift[side])

    def map_copy(who):
        return remote(msend, mbuf.at[who], m_s, m_r.at[who], *own_owner)

    def a_copy(who):
        return remote(asend, abuf.at[who], a_s, a_r.at[who], *own_owner)

    def face_copy(k, side):
        return remote(
            ysend.at[k, side], xbuf.at[k, 1 - side], face_s.at[k, side], face_r.at[k, 1 - side], g, s + shift[side]
        )

    def face_arrival(k, side):
        return remote(ysend.at[k, side], xbuf.at[k, side], face_s.at[k, side], face_r.at[k, side], g, s + shift[side])

    def p_copy(k, side):
        return remote(
            psend.at[k, side], pbuf.at[k, 1 - side, m], p_s.at[k, side], p_r.at[k, 1 - side],
            *side_owner[side],
        )

    def p_local(k, side):
        return pltpu.make_async_copy(psend.at[k, side], pbuf.at[k, 1 - side, m], p_r.at[k, 1 - side])

    def p_start(k, side):
        pl.when(both(has_side[side], jnp.logical_not(to_self[side])))(lambda: p_copy(k, side).start())
        pl.when(both(has_side[side], to_self[side]))(lambda: p_local(k, side).start())

    def p_arrival(k, side):
        return remote(pbuf.at[k, side], pbuf.at[k, side], p_s.at[k, side], p_r.at[k, side], g, s + shift[side])

    def owner_copy(k, side):
        return remote(
            esend.at[k], obuf.at[k, 1 - side], o_s.at[k, side], o_r.at[k, 1 - side], *near_owner[side]
        )

    def owner_arrival(k, side):
        return remote(esend.at[k], obuf.at[k, side], o_s.at[k, side], o_r.at[k, side], g, s + shift[side])

    def entry_copy(k, side, q):
        return remote(
            esend.at[k, q], ebuf.at[k, 1 - side], e_s.at[k, side, q], e_r.at[k, 1 - side],
            block * NB + q, owned + shift[side],
        )

    def entry_local(k, side, q):
        return pltpu.make_async_copy(esend.at[k, q], ebuf.at[k, 1 - side], e_r.at[k, 1 - side])

    def entry_self(side, q):
        return both(owned + shift[side] == s, m == q)

    def entry_arrival(k, side):
        return remote(esend.at[k, 0], ebuf.at[k, side], e_s.at[k, side], e_r.at[k, side], g, s + shift[side])

    def carry_copy(k):
        return remote(csend.at[k], cin.at[k], c_s.at[k], c_r.at[k], g + NB, s)

    def last_copy(q):
        return remote(esend.at[SWEEPS - 1, q], efin, fin_s.at[q], fin_r, block * NB + q, owned)

    pl.when(not_own)(lambda: map_copy(m).start())
    for side in range(2):
        pl.when(has_side[side])(lambda: h_copy(side).start())
    for side in range(2):
        pl.when(has_side[side])(lambda: face_copy(0, side).start())

    def owner_finish(k, final):
        pl.when(has_up)(lambda: carry_copy(k).wait_recv())
        carried = twice(cin[k])
        out = local[NB * FACE :] + mm(d_all[NB * FACE :], carried)

        @pl.when(has_down)
        def _():
            csend[k] = out.astype(BF16)
            carry_copy(k).start()

        entries = (local[: NB * FACE] + mm(d_all[: NB * FACE], carried)).astype(BF16)
        for q in range(NB):
            esend[k, q] = entries[q * FACE : q * FACE + FACE]
        if final:
            for q in range(NB):
                pl.when(jnp.logical_not(both(owned == s, m == q)))(lambda: last_copy(q).start())

            @pl.when(owns_own)
            def _():
                efin[...] = esend[k, m]
        else:
            for side in range(2):
                @pl.when(owned_side[side])
                def _():
                    for q in range(NB):
                        pl.when(jnp.logical_not(entry_self(side, q)))(lambda: entry_copy(k, side, q).start())
                        pl.when(entry_self(side, q))(lambda: entry_local(k, side, q).start())
            for side in range(2):
                pl.when(owned_side[side])(lambda: owner_copy(k, side).start())

    @pl.when(is_owner)
    def _():
        for q in range(NB):
            pl.when(jnp.logical_not(both(owned == s, m == q)))(lambda: map_copy(q).wait_recv())
        eye = (
            lax.broadcasted_iota(jnp.int32, (FACE, FACE), 0) == lax.broadcasted_iota(jnp.int32, (FACE, FACE), 1)
        ).astype(F32)
        none = jnp.zeros((FACE, FACE), F32)
        state = jnp.concatenate([none] * NB + [eye], axis=1)
        for q in range(NB + 1):
            m_all[q * FACE : q * FACE + FACE] = left_pair(state[:, : NB * FACE])
            d_all[q * FACE : q * FACE + FACE] = left_pair(state[:, NB * FACE :])
            if q < NB:
                state = mm_fine(mbuf[q, :64], state) + jnp.concatenate(
                    [eye if r == q else none for r in range(NB)] + [none], axis=1
                )
        starts = jnp.concatenate([mbuf[q, 64:] for q in range(NB)], axis=0)
        local[...] = mm(m_all[...], twice(starts))
        pl.when(jnp.logical_not(has_up))(lambda: owner_finish(0, False))

    for side in range(2):
        pl.when(has_side[side])(lambda: h_arrival(side).wait_recv())
    from_o = [jnp.concatenate([hbuf[side, :64], hbuf[side, 64:128]], axis=1) for side in range(2)]
    from_fe = [jnp.concatenate([hbuf[side, 128:, :64], hbuf[side, 128:, 64:]], axis=0) for side in range(2)]
    for side in range(2):
        at = 128 + side * EL * FACE
        pf_const[64 * side : 64 * side + 64] = mm(from_o[side], pf_const[at : at + 256].astype(BF16))
        psend[0, side] = pf_const[64 * side : 64 * side + 64].astype(BF16)
        p_start(0, side)
    asend[...] = jnp.concatenate([mm(own_o[side], from_fe[side]) for side in range(2)], axis=1).astype(BF16)
    pl.when(not_own)(lambda: a_copy(m).start())

    @pl.when(owns_own)
    def _():
        abuf[m] = asend[...]

    blank = jnp.zeros((FACE, FACE), BF16)
    for side in range(2):
        at = 128 + side * EL * FACE
        pf_mat[64 * side : 64 * side + 64] = mm(from_o[side], pf_mat[at : at + 256]).astype(BF16)
        for p in range(EL):
            part = from_fe[side][p * FACE : p * FACE + FACE]
            row = 128 * p + 64 * side
            fe_next[row : row + FACE] = jnp.concatenate([part, blank] if side == 0 else [blank, part], axis=1)

    @pl.when(is_owner)
    def _():
        pl.when(has_up)(lambda: owner_finish(0, False))
        for q in range(NB):
            pl.when(jnp.logical_not(both(owned == s, m == q)))(lambda: a_copy(q).wait_recv())

    def owner_gather(k):
        for side in range(2):
            @pl.when(owned_side[side])
            def _():
                p_arrival(k, side).wait_recv()
                owner_arrival(k, side).wait_recv()
        offsets = []
        for q in range(NB):
            known = mbuf[q, 64:].astype(F32) + pbuf[k, 0, q].astype(F32) + pbuf[k, 1, q].astype(F32)
            coming = jnp.concatenate([obuf[k, 0, q], obuf[k, 1, q]], axis=0)
            offsets.append((known + mm(abuf[q], coming)).astype(BF16))
        local[...] = mm(m_all[...], twice(jnp.concatenate(offsets, axis=0)))

    def member_gather(k):
        for side in range(2):
            @pl.when(has_side[side])
            def _():
                entry_arrival(k, side).wait_recv()
                face_arrival(k, side).wait_recv()
        early = jnp.concatenate([xbuf[k, side, p] for p in range(EL) for side in range(2)], axis=0)
        entries = jnp.concatenate([ebuf[k, 0], ebuf[k, 1]], axis=0)
        now = (early.astype(F32) + mm(fe_next[...], entries)).astype(BF16)
        for p in range(EL):
            xs[p] = now[128 * p : 128 * p + 128]
        return now

    @pl.loop(0, SWEEPS - 2)
    def _(k):
        now = member_gather(k)
        for side in range(2):
            at = 128 + side * EL * FACE
            ahead = (mm(pf_mat[at : at + 256], now) + pf_const[at : at + 256]).astype(BF16)
            for p in range(EL):
                ysend[k + 1, side, p] = ahead[p * FACE : p * FACE + FACE]
            pl.when(has_side[side])(lambda: face_copy(k + 1, side).start())
        ahead = (mm(pf_mat[:128], now) + pf_const[:128]).astype(BF16)
        for side in range(2):
            psend[k + 1, side] = ahead[64 * side : 64 * side + 64]
            p_start(k + 1, side)
        @pl.when(is_owner)
        def _():
            owner_gather(k)
            owner_finish(k + 1, False)

    last = SWEEPS - 1

    @pl.when(is_owner)
    def _():
        owner_gather(last - 1)
        owner_finish(last, True)

    now = member_gather(last - 1)
    places = []
    for t in range(EL):
        place = jnp.int32(0)
        for p in range(1, EL):
            place = jnp.where(slots[p] == t, p, place)
        places.append(place)
    traces = mm(s_mat[...], now) + s_const[...]
    for t in range(EL):
        pre_out[t] = gain_full[t] + mm(side_full[t], xs[places[t]])
    pl.when(not_own)(lambda: last_copy(m).wait_recv())
    entry = efin[...]
    traces = (traces + mm(se_mat[...], twice(entry))).astype(BF16)
    inflow[0] = entry
    for p in range(1, EL):
        inflow[p] = traces[(p - 1) * FACE : p * FACE]

    def out_copy(t):
        return pltpu.make_async_copy(out_v.at[t], out_hbm.at[t], out_sem.at[t])

    for t in range(EL):
        out_v[t] = (pre_out[t] + mm(lift_full[t], twice(inflow[places[t]]))).astype(BF16)
        out_copy(t).start()

    @pl.when(not_own)
    def _():
        map_copy(m).wait_send()
        a_copy(m).wait_send()

    for side in range(2):
        pl.when(has_side[side])(lambda: h_copy(side).wait_send())

    @pl.loop(0, SWEEPS - 1)
    def _(k):
        for side in range(2):
            pl.when(has_side[side])(lambda: face_copy(k, side).wait_send())
            pl.when(both(has_side[side], jnp.logical_not(to_self[side])))(lambda: p_copy(k, side).wait_send())

            @pl.when(both(is_owner, owned_side[side]))
            def _():
                owner_copy(k, side).wait_send()
                for q in range(NB):
                    pl.when(jnp.logical_not(entry_self(side, q)))(lambda: entry_copy(k, side, q).wait_send())

    @pl.when(is_owner)
    def _():
        @pl.when(has_down)
        def _():
            @pl.loop(0, SWEEPS)
            def _(k):
                carry_copy(k).wait_send()

        for q in range(NB):
            pl.when(jnp.logical_not(both(owned == s, m == q)))(lambda: last_copy(q).wait_send())

    for t in range(EL):
        out_copy(t).wait()


def shards(blocks_along, spans, right_sides, inverse, coupling, sweep_order):
    vmem = pltpu.VMEM
    dma = pltpu.SemaphoreType.DMA
    hbm = pl.BlockSpec(memory_space=pltpu.HBM)
    trips = SWEEPS - 1
    placed = pl.pallas_call(
        lambda *refs: kernel(blocks_along, spans, *refs),
        name="sweeps",
        out_shape=jax.ShapeDtypeStruct((EL, NODES, RHS), BF16),
        in_specs=[pl.BlockSpec(memory_space=pltpu.SMEM), hbm, hbm, hbm],
        out_specs=hbm,
        scratch_shapes=[
            vmem((EL, NODES, RHS), BF16),
            vmem((EL, NODES, NODES), BF16),
            vmem((EL, 3 * FACE, NODES), BF16),
            vmem((EL, NODES, RHS), BF16),
            vmem((EL, NODES, 2 * FACE), BF16),
            vmem((EL, NODES, 2 * FACE), BF16),
            vmem((EL, NODES, RHS), F32),
            vmem((EL, 3 * FACE, 2 * FACE), BF16),
            vmem((EL, 3 * FACE, 2 * FACE), F32),
            vmem((EL, 3 * FACE, RHS), F32),
            vmem((640, 512), BF16),
            vmem((640, RHS), F32),
            vmem((512, 128), BF16),
            vmem((3 * FACE, 512), BF16),
            vmem((3 * FACE, 2 * FACE), BF16),
            vmem((3 * FACE, RHS), F32),
            vmem(((NB + 1) * FACE, 2 * NB * FACE), BF16),
            vmem(((NB + 1) * FACE, 2 * FACE), BF16),
            vmem(((NB + 1) * FACE, RHS), F32),
            vmem((EL, FACE, RHS), BF16),
            vmem((EL, 2 * FACE, RHS), BF16),
            vmem((EL, NODES, RHS), F32),
            vmem((2, 256, 128), BF16),
            vmem((2, 256, 128), BF16),
            vmem((128, 128), BF16),
            vmem((FACE, 128), BF16),
            vmem((NB, 128, 128), BF16),
            vmem((NB, FACE, 128), BF16),
            vmem((trips, 2, EL, FACE, RHS), BF16),
            vmem((trips, 2, EL, FACE, RHS), BF16),
            vmem((trips, 2, FACE, RHS), BF16),
            vmem((trips, 2, NB, FACE, RHS), BF16),
            vmem((SWEEPS, NB, FACE, RHS), BF16),
            vmem((trips, 2, NB, FACE, RHS), BF16),
            vmem((trips, 2, FACE, RHS), BF16),
            vmem((SWEEPS, FACE, RHS), BF16),
            vmem((SWEEPS, FACE, RHS), BF16),
            vmem((FACE, RHS), BF16),
            dma((EL, 3)),
            dma((EL,)),
            dma((2,)),
            dma((2,)),
            dma,
            dma((NB,)),
            dma,
            dma((NB,)),
            dma((trips, 2)),
            dma((trips, 2)),
            dma((trips, 2, NB)),
            dma((trips, 2)),
            dma((trips, 2)),
            dma((trips, 2)),
            dma((trips, 2)),
            dma((trips, 2)),
            dma((SWEEPS,)),
            dma((SWEEPS,)),
            dma((NB,)),
            dma,
        ],
        compiler_params=pltpu.CompilerParams(
            collective_id=0, has_side_effects=True, vmem_limit_bytes=58 * 2**20
        ),
    )(
        sweep_order[0, 0],
        right_sides[0, 0],
        inverse[0, 0],
        coupling[0, 0].reshape(EL, 3 * FACE, NODES),
    )
    return placed[None, None]


def solution(mesh):
    blocks_along = mesh.shape["stream"] // NB
    spans = mesh.shape["span"]
    in_specs = (
        P("stream", "span", None, None, None),
        P("stream", "span", None, None, None),
        P("stream", "span", None, None, None, None),
        P("stream", "span", None),
    )
    out_specs = P("stream", "span", None, None, None)

    def run(right_sides, inverse, coupling, sweep_order):
        return shards(blocks_along, spans, right_sides, inverse, coupling, sweep_order)

    return jax.shard_map(run, mesh=mesh, in_specs=in_specs, out_specs=out_specs, check_vma=False)
```

```python
import jax
import jax.numpy as jnp
from jax import lax
from jax.experimental import pallas as pl
from jax.experimental.pallas import tpu as pltpu
from jax.sharding import PartitionSpec as P

SWEEPS = 6
EL = 4
NODES = 512
FACE = 64
RHS = 128
NB = 4
F32 = jnp.float32
BF16 = jnp.bfloat16
MESH = pl.DeviceIdType.MESH


def mm(left, right):
    return jnp.dot(left, right, preferred_element_type=F32)


def mm_nt(left, right):
    return lax.dot_general(left, right, (((1,), (1,)), ((), ())), preferred_element_type=F32)


def split(value):
    high = value.astype(BF16)
    return high, (value - high.astype(F32)).astype(BF16)


def left_pair(value):
    return jnp.concatenate(split(value), axis=1)


def twice(value):
    return jnp.concatenate([value, value], axis=0)


def mm_fine(pair, right):
    high, low = split(right)
    return mm(
        jnp.concatenate([pair, pair[:, :FACE]], axis=1),
        jnp.concatenate([high, high, low], axis=0),
    )


def face_groups(values):
    lower = [values[64 * a : 64 * a + 16] for a in range(8)]
    upper = [values[64 * a + 48 : 64 * a + 64] for a in range(8)]
    return jnp.concatenate([values[NODES - FACE :]] + lower + upper, axis=0)


def faces_of(values):
    lower = [values[64 + 16 * a : 64 + 16 * a + 8] for a in range(8)]
    upper = [values[192 + 16 * a + 8 : 192 + 16 * a + 16] for a in range(8)]
    return jnp.concatenate([values[:FACE]] + lower + upper, axis=0)


def kernel(
    blocks_along, spans,
    order_ref, rs_hbm, inv_hbm, cpl_hbm,
    out_hbm,
    rs, inv, cpl, out_v,
    lift_full, side_full, gain_full, lift_face, side_face, gain_face,
    pf_mat, pf_const, fe_next, s_mat, se_mat, s_const,
    m_all, d_all, local, inflow, xs, pre_out,
    hsend, hbuf, msend, asend, mbuf, abuf, xbuf, ysend, ebuf, obuf, esend, pbuf, psend, cin, csend, tin, tsend, chain, running, efin,
    in_sem, out_sem, h_s, h_r, m_s, m_r, a_s, a_r,
    face_s, face_r, e_s, e_r, o_s, o_r, p_s, p_r, c_s, c_r, t_s, t_r, fin_s, fin_r,
):
    g = lax.axis_index("stream")
    s = lax.axis_index("span")
    block = g // NB
    m = g % NB

    odd = s % 2

    def owner_of(column):
        return block * NB + (NB - 1) * (column % 2), column - column % 2 + 1

    first_place = (m == 0).astype(jnp.int32)
    is_owner = jnp.logical_and(odd == 1, jnp.logical_or(m == 0, m == NB - 1))
    owned = s - first_place * odd
    owns_other = jnp.logical_and(is_owner, owned != s)
    owns_own = jnp.logical_and(is_owner, owned == s)
    has_up = block > 0
    has_side = (s > 0, s < spans - 1)
    owned_side = (owned > 0, owned < spans - 1)
    shift = (-1, 1)
    side_owner = (owner_of(s + 15), owner_of(s + 17))
    side_owner = tuple((a, b - 16) for a, b in side_owner)
    near_owner = tuple((a, b - 16) for a, b in (owner_of(owned + 15), owner_of(owned + 17)))
    own_owner = owner_of(s)
    to_self = (owns_other, jnp.bool_(False))

    def in_copies(t):
        return [
            pltpu.make_async_copy(inv_hbm.at[t], inv.at[t], in_sem.at[t, 0]),
            pltpu.make_async_copy(cpl_hbm.at[t], cpl.at[t], in_sem.at[t, 1]),
            pltpu.make_async_copy(rs_hbm.at[t], rs.at[t], in_sem.at[t, 2]),
        ]

    for t in range(EL):
        for c in in_copies(t):
            c.start()

    barrier = pltpu.get_barrier_semaphore()

    def greet(a, b):
        pl.semaphore_signal(barrier, inc=1, device_id=(a, b), device_id_type=MESH)

    def both(a, b):
        return jnp.logical_and(a, b)

    not_owner = jnp.logical_not(is_owner)
    not_own = jnp.logical_not(owns_own)
    for side in range(2):
        @pl.when(has_side[side])
        def _():
            greet(g, s + shift[side])

            @pl.when(jnp.logical_not(to_self[side]))
            def _():
                greet(*side_owner[side])

        @pl.when(both(is_owner, owned_side[side]))
        def _():
            greet(*near_owner[side])
            for q in range(NB):
                @pl.when(jnp.logical_not(both(owned + shift[side] == s, m == q)))
                def _():
                    greet(block * NB + q, owned + shift[side])

        @pl.when(jnp.logical_not(has_side[side]))
        def _():
            hbuf[side] = jnp.zeros((256, 128), BF16)
            for k in range(SWEEPS - 1):
                xbuf[k, side] = jnp.zeros((EL, FACE, RHS), BF16)
                ebuf[k, side] = jnp.zeros((FACE, RHS), BF16)

        @pl.when(both(is_owner, jnp.logical_not(owned_side[side])))
        def _():
            for k in range(SWEEPS - 1):
                obuf[k, side] = jnp.zeros((NB, FACE, RHS), BF16)
                pbuf[k, side] = jnp.zeros((NB, FACE, RHS), BF16)

    @pl.when(is_owner)
    def _():
        for q in range(NB):
            pl.when(jnp.logical_not(both(owned == s, m == q)))(lambda: greet(block * NB + q, owned))
        for i in range(1, blocks_along):
            greet((g + i * NB) % (blocks_along * NB), s)

    pl.when(not_own)(lambda: greet(*own_owner))

    before = blocks_along - 1
    for j in range(before):
        @pl.when(both(is_owner, j >= block))
        def _():
            chain[:, j * FACE : j * FACE + FACE] = jnp.zeros((FACE, FACE), BF16)
            chain[:, (before + j) * FACE : (before + j) * FACE + FACE] = jnp.zeros((FACE, FACE), BF16)
            for k in range(SWEEPS):
                cin[k, j] = jnp.zeros((FACE, RHS), BF16)

    for t in range(EL):
        for c in in_copies(t):
            c.wait()
        rows = face_groups(inv[t])
        chosen = faces_of(mm_nt(rows, cpl[t]))
        lift_face[t] = left_pair(chosen[:, :FACE])
        side_face[t] = chosen[:, FACE:]
        gain_face[t] = faces_of(mm(rows, rs[t]))

    slots = [order_ref[p] for p in range(EL)]
    trace = None
    pf_mat[...] = jnp.zeros(pf_mat.shape, BF16)
    s_mat[...] = jnp.zeros(s_mat.shape, BF16)
    face_entry = [[None] * EL, [None] * EL]
    for p in range(EL):
        lift = lift_face[slots[p]]
        side = side_face[slots[p]]
        gain = gain_face[slots[p]]
        if p == 0:
            lift_own = lift[:, :FACE].astype(F32) + lift[:, FACE:].astype(F32)
            result = jnp.concatenate([side, gain, lift_own], axis=1)
        else:
            moved = mm_fine(lift, trace)
            result = jnp.concatenate(
                [moved[:, : 128 * p], side, moved[:, 128 * p : 128 * p + 128] + gain, moved[:, 128 * p + 128 :]],
                axis=1,
            )
        wide = 128 * (p + 1)
        for layer in range(2):
            at = 128 + layer * EL * FACE + p * FACE
            part = result[FACE + layer * FACE : 2 * FACE + layer * FACE]
            pf_mat[at : at + FACE, :wide] = part[:, :wide].astype(BF16)
            pf_const[at : at + FACE] = part[:, wide : wide + 128]
            face_entry[layer][p] = part[:, wide + 128 :].astype(BF16)
            ysend[0, layer, p] = part[:, wide : wide + 128].astype(BF16)
        trace = result[:FACE]
        if p < EL - 1:
            s_mat[p * FACE : p * FACE + FACE, :wide] = trace[:, :wide].astype(BF16)
            s_const[p * FACE : p * FACE + FACE] = trace[:, wide : wide + 128]
            se_mat[p * FACE : p * FACE + FACE] = left_pair(trace[:, wide + 128 :])
    own_o = [
        jnp.concatenate([trace[:, 128 * p + 64 * side : 128 * p + 64 * side + 64] for p in range(EL)], axis=1).astype(BF16)
        for side in range(2)
    ]
    for side in range(2):
        fe = face_entry[side]
        hsend[side, :64] = own_o[side][:, :128]
        hsend[side, 64:128] = own_o[side][:, 128:]
        hsend[side, 128:] = jnp.concatenate(
            [jnp.concatenate([fe[0], fe[1]], axis=0), jnp.concatenate([fe[2], fe[3]], axis=0)], axis=1
        )
    msend[:64] = left_pair(trace[:, 640:])
    msend[64:] = trace[:, 512:640].astype(BF16)

    @pl.when(owns_own)
    def _():
        mbuf[m] = msend[...]

    def number(flag):
        return flag.astype(jnp.int32)

    greetings = 2 * (number(has_side[0]) + number(has_side[1])) - number(owns_other) + number(not_own)
    greetings = greetings + number(is_owner) * (
        (NB + 1) * (number(owned_side[0]) + number(owned_side[1]))
        + NB + blocks_along - 1
    ) - number(owns_other) - number(owns_own)
    pl.semaphore_wait(barrier, greetings)

    def remote(src, dst, send, recv, a, b):
        return pltpu.make_async_remote_copy(src, dst, send, recv, device_id=(a, b), device_id_type=MESH)

    def h_copy(side):
        return remote(hsend.at[side], hbuf.at[1 - side], h_s.at[side], h_r.at[1 - side], g, s + shift[side])

    def h_arrival(side):
        return remote(hsend.at[side], hbuf.at[side], h_s.at[side], h_r.at[side], g, s + shift[side])

    def map_copy(who):
        return remote(msend, mbuf.at[who], m_s, m_r.at[who], *own_owner)

    def a_copy(who):
        return remote(asend, abuf.at[who], a_s, a_r.at[who], *own_owner)

    def face_copy(k, side):
        return remote(
            ysend.at[k, side], xbuf.at[k, 1 - side], face_s.at[k, side], face_r.at[k, 1 - side], g, s + shift[side]
        )

    def face_arrival(k, side):
        return remote(ysend.at[k, side], xbuf.at[k, side], face_s.at[k, side], face_r.at[k, side], g, s + shift[side])

    def p_copy(k, side):
        return remote(
            psend.at[k, side], pbuf.at[k, 1 - side, m], p_s.at[k, side], p_r.at[k, 1 - side],
            *side_owner[side],
        )

    def p_local(k, side):
        return pltpu.make_async_copy(psend.at[k, side], pbuf.at[k, 1 - side, m], p_r.at[k, 1 - side])

    def p_start(k, side):
        pl.when(both(has_side[side], jnp.logical_not(to_self[side])))(lambda: p_copy(k, side).start())
        pl.when(both(has_side[side], to_self[side]))(lambda: p_local(k, side).start())

    def p_arrival(k, side):
        return remote(pbuf.at[k, side], pbuf.at[k, side], p_s.at[k, side], p_r.at[k, side], g, s + shift[side])

    def owner_copy(k, side):
        return remote(
            esend.at[k], obuf.at[k, 1 - side], o_s.at[k, side], o_r.at[k, 1 - side], *near_owner[side]
        )

    def owner_arrival(k, side):
        return remote(esend.at[k], obuf.at[k, side], o_s.at[k, side], o_r.at[k, side], g, s + shift[side])

    def entry_copy(k, side, q):
        return remote(
            esend.at[k, q], ebuf.at[k, 1 - side], e_s.at[k, side, q], e_r.at[k, 1 - side],
            block * NB + q, owned + shift[side],
        )

    def entry_local(k, side, q):
        return pltpu.make_async_copy(esend.at[k, q], ebuf.at[k, 1 - side], e_r.at[k, 1 - side])

    def entry_self(side, q):
        return both(owned + shift[side] == s, m == q)

    def entry_arrival(k, side):
        return remote(esend.at[k, 0], ebuf.at[k, side], e_s.at[k, side], e_r.at[k, side], g, s + shift[side])

    def rest_copy(k, ahead):
        return remote(
            csend.at[k], cin.at[k, block], c_s.at[k, ahead - 1], c_r.at[k, block], g + ahead * NB, s
        )

    def rest_arrival(k, j):
        return remote(csend.at[k], cin.at[k, j], c_s.at[k, 0], c_r.at[k, j], g, s)

    def turn_copy(ahead):
        return remote(tsend, tin.at[block], t_s.at[ahead - 1], t_r.at[block], g + ahead * NB, s)

    def turn_arrival(j):
        return remote(tsend, tin.at[j], t_s.at[0], t_r.at[j], g, s)

    def later(ahead):
        return block + ahead < blocks_along

    def send_rest(k):
        csend[k] = local[NB * FACE :].astype(BF16)
        for ahead in range(1, blocks_along):
            pl.when(later(ahead))(lambda: rest_copy(k, ahead).start())

    def form_chain():
        eye = (
            lax.broadcasted_iota(jnp.int32, (FACE, FACE), 0) == lax.broadcasted_iota(jnp.int32, (FACE, FACE), 1)
        ).astype(F32)
        for j in reversed(range(before)):
            @pl.when(j + 1 == block)
            def _():
                running[...] = left_pair(eye)

            if j + 1 < before:
                @pl.when(j + 1 < block)
                def _():
                    turn_arrival(j + 1).wait_recv()
                    turn = tin[j + 1, :, :FACE].astype(F32) + tin[j + 1, :, FACE:].astype(F32)
                    running[...] = left_pair(mm_fine(running[...], turn))

            @pl.when(j < block)
            def _():
                chain[:, j * FACE : j * FACE + FACE] = running[:, :FACE]
                chain[:, (before + j) * FACE : (before + j) * FACE + FACE] = running[:, FACE:]

        pl.when(has_up)(lambda: turn_arrival(0).wait_recv())

    def last_copy(q):
        return remote(esend.at[SWEEPS - 1, q], efin, fin_s.at[q], fin_r, block * NB + q, owned)

    pl.when(not_own)(lambda: map_copy(m).start())
    for side in range(2):
        pl.when(has_side[side])(lambda: h_copy(side).start())
    for side in range(2):
        pl.when(has_side[side])(lambda: face_copy(0, side).start())

    for t in range(EL):
        maps = mm_nt(inv[t], cpl[t])
        lift_full[t] = left_pair(maps[:, :FACE])
        side_full[t] = maps[:, FACE:].astype(BF16)
        gain_full[t] = mm(inv[t], rs[t])

    def owner_finish(k, final):
        for j in range(before):
            pl.when(j < block)(lambda: rest_arrival(k, j).wait_recv())
        rests = jnp.concatenate([cin[k, j] for j in range(before)], axis=0)
        carried = twice(mm(chain[...], twice(rests)).astype(BF16))
        entries = (local[: NB * FACE] + mm(d_all[: NB * FACE], carried)).astype(BF16)
        for q in range(NB):
            esend[k, q] = entries[q * FACE : q * FACE + FACE]
        if final:
            for q in range(NB):
                pl.when(jnp.logical_not(both(owned == s, m == q)))(lambda: last_copy(q).start())

            @pl.when(owns_own)
            def _():
                efin[...] = esend[k, m]
        else:
            for side in range(2):
                @pl.when(owned_side[side])
                def _():
                    for q in range(NB):
                        pl.when(jnp.logical_not(entry_self(side, q)))(lambda: entry_copy(k, side, q).start())
                        pl.when(entry_self(side, q))(lambda: entry_local(k, side, q).start())
            for side in range(2):
                pl.when(owned_side[side])(lambda: owner_copy(k, side).start())

    @pl.when(is_owner)
    def _():
        for q in range(NB):
            pl.when(jnp.logical_not(both(owned == s, m == q)))(lambda: map_copy(q).wait_recv())
        eye = (
            lax.broadcasted_iota(jnp.int32, (FACE, FACE), 0) == lax.broadcasted_iota(jnp.int32, (FACE, FACE), 1)
        ).astype(F32)
        none = jnp.zeros((FACE, FACE), F32)
        state = jnp.concatenate([none] * NB + [eye], axis=1)
        for q in range(NB + 1):
            m_all[q * FACE : q * FACE + FACE] = left_pair(state[:, : NB * FACE])
            d_all[q * FACE : q * FACE + FACE] = left_pair(state[:, NB * FACE :])
            if q < NB:
                state = mm_fine(mbuf[q, :64], state) + jnp.concatenate(
                    [eye if r == q else none for r in range(NB)] + [none], axis=1
                )
        tsend[...] = d_all[NB * FACE :]
        for ahead in range(1, blocks_along):
            pl.when(later(ahead))(lambda: turn_copy(ahead).start())
        starts = jnp.concatenate([mbuf[q, 64:] for q in range(NB)], axis=0)
        local[...] = mm(m_all[...], twice(starts))
        send_rest(0)
        pl.when(jnp.logical_not(has_up))(lambda: owner_finish(0, False))

    for side in range(2):
        pl.when(has_side[side])(lambda: h_arrival(side).wait_recv())
    from_o = [jnp.concatenate([hbuf[side, :64], hbuf[side, 64:128]], axis=1) for side in range(2)]
    from_fe = [jnp.concatenate([hbuf[side, 128:, :64], hbuf[side, 128:, 64:]], axis=0) for side in range(2)]
    for side in range(2):
        at = 128 + side * EL * FACE
        pf_const[64 * side : 64 * side + 64] = mm(from_o[side], pf_const[at : at + 256].astype(BF16))
        psend[0, side] = pf_const[64 * side : 64 * side + 64].astype(BF16)
        p_start(0, side)
    asend[...] = jnp.concatenate([mm(own_o[side], from_fe[side]) for side in range(2)], axis=1).astype(BF16)
    pl.when(not_own)(lambda: a_copy(m).start())

    @pl.when(owns_own)
    def _():
        abuf[m] = asend[...]

    blank = jnp.zeros((FACE, FACE), BF16)
    for side in range(2):
        at = 128 + side * EL * FACE
        pf_mat[64 * side : 64 * side + 64] = mm(from_o[side], pf_mat[at : at + 256]).astype(BF16)
        for p in range(EL):
            part = from_fe[side][p * FACE : p * FACE + FACE]
            row = 128 * p + 64 * side
            fe_next[row : row + FACE] = jnp.concatenate([part, blank] if side == 0 else [blank, part], axis=1)

    @pl.when(is_owner)
    def _():
        @pl.when(has_up)
        def _():
            form_chain()
            owner_finish(0, False)

        for q in range(NB):
            pl.when(jnp.logical_not(both(owned == s, m == q)))(lambda: a_copy(q).wait_recv())

    def owner_gather(k):
        for side in range(2):
            @pl.when(owned_side[side])
            def _():
                p_arrival(k, side).wait_recv()
                owner_arrival(k, side).wait_recv()
        offsets = []
        for q in range(NB):
            known = mbuf[q, 64:].astype(F32) + pbuf[k, 0, q].astype(F32) + pbuf[k, 1, q].astype(F32)
            coming = jnp.concatenate([obuf[k, 0, q], obuf[k, 1, q]], axis=0)
            offsets.append((known + mm(abuf[q], coming)).astype(BF16))
        local[...] = mm(m_all[...], twice(jnp.concatenate(offsets, axis=0)))
        send_rest(k + 1)

    def member_gather(k):
        for side in range(2):
            @pl.when(has_side[side])
            def _():
                entry_arrival(k, side).wait_recv()
                face_arrival(k, side).wait_recv()
        early = jnp.concatenate([xbuf[k, side, p] for p in range(EL) for side in range(2)], axis=0)
        entries = jnp.concatenate([ebuf[k, 0], ebuf[k, 1]], axis=0)
        now = (early.astype(F32) + mm(fe_next[...], entries)).astype(BF16)
        for p in range(EL):
            xs[p] = now[128 * p : 128 * p + 128]
        return now

    @pl.loop(0, SWEEPS - 2)
    def _(k):
        now = member_gather(k)
        for side in range(2):
            at = 128 + side * EL * FACE
            ahead = (mm(pf_mat[at : at + 256], now) + pf_const[at : at + 256]).astype(BF16)
            for p in range(EL):
                ysend[k + 1, side, p] = ahead[p * FACE : p * FACE + FACE]
            pl.when(has_side[side])(lambda: face_copy(k + 1, side).start())
        ahead = (mm(pf_mat[:128], now) + pf_const[:128]).astype(BF16)
        for side in range(2):
            psend[k + 1, side] = ahead[64 * side : 64 * side + 64]
            p_start(k + 1, side)
        @pl.when(is_owner)
        def _():
            owner_gather(k)
            owner_finish(k + 1, False)

    last = SWEEPS - 1

    @pl.when(is_owner)
    def _():
        owner_gather(last - 1)
        owner_finish(last, True)

    now = member_gather(last - 1)
    places = []
    for t in range(EL):
        place = jnp.int32(0)
        for p in range(1, EL):
            place = jnp.where(slots[p] == t, p, place)
        places.append(place)
    traces = mm(s_mat[...], now) + s_const[...]
    for t in range(EL):
        pre_out[t] = gain_full[t] + mm(side_full[t], xs[places[t]])
    pl.when(not_own)(lambda: last_copy(m).wait_recv())
    entry = efin[...]
    traces = (traces + mm(se_mat[...], twice(entry))).astype(BF16)
    inflow[0] = entry
    for p in range(1, EL):
        inflow[p] = traces[(p - 1) * FACE : p * FACE]

    def out_copy(t):
        return pltpu.make_async_copy(out_v.at[t], out_hbm.at[t], out_sem.at[t])

    for t in range(EL):
        out_v[t] = (pre_out[t] + mm(lift_full[t], twice(inflow[places[t]]))).astype(BF16)
        out_copy(t).start()

    @pl.when(not_own)
    def _():
        map_copy(m).wait_send()
        a_copy(m).wait_send()

    for side in range(2):
        pl.when(has_side[side])(lambda: h_copy(side).wait_send())

    @pl.loop(0, SWEEPS - 1)
    def _(k):
        for side in range(2):
            pl.when(has_side[side])(lambda: face_copy(k, side).wait_send())
            pl.when(both(has_side[side], jnp.logical_not(to_self[side])))(lambda: p_copy(k, side).wait_send())

            @pl.when(both(is_owner, owned_side[side]))
            def _():
                owner_copy(k, side).wait_send()
                for q in range(NB):
                    pl.when(jnp.logical_not(entry_self(side, q)))(lambda: entry_copy(k, side, q).wait_send())

    @pl.when(is_owner)
    def _():
        for ahead in range(1, blocks_along):
            @pl.when(later(ahead))
            def _():
                turn_copy(ahead).wait_send()

                @pl.loop(0, SWEEPS)
                def _(k):
                    rest_copy(k, ahead).wait_send()

        for q in range(NB):
            pl.when(jnp.logical_not(both(owned == s, m == q)))(lambda: last_copy(q).wait_send())

    for t in range(EL):
        out_copy(t).wait()


def shards(blocks_along, spans, right_sides, inverse, coupling, sweep_order):
    vmem = pltpu.VMEM
    dma = pltpu.SemaphoreType.DMA
    hbm = pl.BlockSpec(memory_space=pltpu.HBM)
    trips = SWEEPS - 1
    before = blocks_along - 1
    placed = pl.pallas_call(
        lambda *refs: kernel(blocks_along, spans, *refs),
        name="sweeps",
        out_shape=jax.ShapeDtypeStruct((EL, NODES, RHS), BF16),
        in_specs=[pl.BlockSpec(memory_space=pltpu.SMEM), hbm, hbm, hbm],
        out_specs=hbm,
        scratch_shapes=[
            vmem((EL, NODES, RHS), BF16),
            vmem((EL, NODES, NODES), BF16),
            vmem((EL, 3 * FACE, NODES), BF16),
            vmem((EL, NODES, RHS), BF16),
            vmem((EL, NODES, 2 * FACE), BF16),
            vmem((EL, NODES, 2 * FACE), BF16),
            vmem((EL, NODES, RHS), F32),
            vmem((EL, 3 * FACE, 2 * FACE), BF16),
            vmem((EL, 3 * FACE, 2 * FACE), F32),
            vmem((EL, 3 * FACE, RHS), F32),
            vmem((640, 512), BF16),
            vmem((640, RHS), F32),
            vmem((512, 128), BF16),
            vmem((3 * FACE, 512), BF16),
            vmem((3 * FACE, 2 * FACE), BF16),
            vmem((3 * FACE, RHS), F32),
            vmem(((NB + 1) * FACE, 2 * NB * FACE), BF16),
            vmem(((NB + 1) * FACE, 2 * FACE), BF16),
            vmem(((NB + 1) * FACE, RHS), F32),
            vmem((EL, FACE, RHS), BF16),
            vmem((EL, 2 * FACE, RHS), BF16),
            vmem((EL, NODES, RHS), F32),
            vmem((2, 256, 128), BF16),
            vmem((2, 256, 128), BF16),
            vmem((128, 128), BF16),
            vmem((FACE, 128), BF16),
            vmem((NB, 128, 128), BF16),
            vmem((NB, FACE, 128), BF16),
            vmem((trips, 2, EL, FACE, RHS), BF16),
            vmem((trips, 2, EL, FACE, RHS), BF16),
            vmem((trips, 2, FACE, RHS), BF16),
            vmem((trips, 2, NB, FACE, RHS), BF16),
            vmem((SWEEPS, NB, FACE, RHS), BF16),
            vmem((trips, 2, NB, FACE, RHS), BF16),
            vmem((trips, 2, FACE, RHS), BF16),
            vmem((SWEEPS, before, FACE, RHS), BF16),
            vmem((SWEEPS, FACE, RHS), BF16),
            vmem((before, FACE, 128), BF16),
            vmem((FACE, 128), BF16),
            vmem((FACE, 2 * before * FACE), BF16),
            vmem((FACE, 128), BF16),
            vmem((FACE, RHS), BF16),
            dma((EL, 3)),
            dma((EL,)),
            dma((2,)),
            dma((2,)),
            dma,
            dma((NB,)),
            dma,
            dma((NB,)),
            dma((trips, 2)),
            dma((trips, 2)),
            dma((trips, 2, NB)),
            dma((trips, 2)),
            dma((trips, 2)),
            dma((trips, 2)),
            dma((trips, 2)),
            dma((trips, 2)),
            dma((SWEEPS, before)),
            dma((SWEEPS, before)),
            dma((before,)),
            dma((before,)),
            dma((NB,)),
            dma,
        ],
        compiler_params=pltpu.CompilerParams(
            collective_id=0, has_side_effects=True, vmem_limit_bytes=58 * 2**20
        ),
    )(
        sweep_order[0, 0],
        right_sides[0, 0],
        inverse[0, 0],
        coupling[0, 0].reshape(EL, 3 * FACE, NODES),
    )
    return placed[None, None]


def solution(mesh):
    blocks_along = mesh.shape["stream"] // NB
    spans = mesh.shape["span"]
    in_specs = (
        P("stream", "span", None, None, None),
        P("stream", "span", None, None, None),
        P("stream", "span", None, None, None, None),
        P("stream", "span", None),
    )
    out_specs = P("stream", "span", None, None, None)

    def run(right_sides, inverse, coupling, sweep_order):
        return shards(blocks_along, spans, right_sides, inverse, coupling, sweep_order)

    return jax.shard_map(run, mesh=mesh, in_specs=in_specs, out_specs=out_specs, check_vma=False)
```

```python
import jax
import jax.numpy as jnp
from jax import lax
from jax.experimental import pallas as pl
from jax.experimental.pallas import tpu as pltpu
from jax.sharding import PartitionSpec as P

SWEEPS = 6
EL = 4
NODES = 512
FACE = 64
RHS = 128
NB = 4
F32 = jnp.float32
BF16 = jnp.bfloat16
MESH = pl.DeviceIdType.MESH


def mm(left, right):
    return jnp.dot(left, right, preferred_element_type=F32)


def mm_nt(left, right):
    return lax.dot_general(left, right, (((1,), (1,)), ((), ())), preferred_element_type=F32)


def split(value):
    high = value.astype(BF16)
    return high, (value - high.astype(F32)).astype(BF16)


def left_pair(value):
    return jnp.concatenate(split(value), axis=1)


def twice(value):
    return jnp.concatenate([value, value], axis=0)


def mm_fine(pair, right):
    high, low = split(right)
    return mm(
        jnp.concatenate([pair, pair[:, :FACE]], axis=1),
        jnp.concatenate([high, high, low], axis=0),
    )


def face_groups(values):
    lower = [values[64 * a : 64 * a + 16] for a in range(8)]
    upper = [values[64 * a + 48 : 64 * a + 64] for a in range(8)]
    return jnp.concatenate([values[NODES - FACE :]] + lower + upper, axis=0)


def faces_of(values):
    lower = [values[64 + 16 * a : 64 + 16 * a + 8] for a in range(8)]
    upper = [values[192 + 16 * a + 8 : 192 + 16 * a + 16] for a in range(8)]
    return jnp.concatenate([values[:FACE]] + lower + upper, axis=0)


def kernel(
    blocks_along, spans,
    order_ref, rs_hbm, inv_hbm, cpl_hbm,
    out_hbm,
    rs, inv, cpl, out_v,
    lift_full, side_full, gain_full, lift_face, side_face, gain_face,
    pf_mat, pf_const, fe_next, s_mat, se_mat, s_const,
    m_all, d_all, local, inflow, xs, pre_out,
    hsend, hbuf, msend, asend, mbuf, abuf, xbuf, ysend, ebuf, obuf, esend, pbuf, psend, cin, csend, tin, tsend, chain, running, efin,
    in_sem, out_sem, h_s, h_r, m_s, m_r, a_s, a_r,
    face_s, face_r, e_s, e_r, o_s, o_r, p_s, p_r, c_s, c_r, t_s, t_r, fin_s, fin_r,
):
    g = lax.axis_index("stream")
    s = lax.axis_index("span")
    block = g // NB
    m = g % NB

    odd = s % 2

    def owner_of(column):
        return block * NB + (NB - 1) * (column % 2), column - column % 2 + 1

    first_place = (m == 0).astype(jnp.int32)
    is_owner = jnp.logical_and(odd == 1, jnp.logical_or(m == 0, m == NB - 1))
    owned = s - first_place * odd
    owns_other = jnp.logical_and(is_owner, owned != s)
    owns_own = jnp.logical_and(is_owner, owned == s)
    has_up = block > 0
    has_side = (s > 0, s < spans - 1)
    owned_side = (owned > 0, owned < spans - 1)
    shift = (-1, 1)
    side_owner = (owner_of(s + 15), owner_of(s + 17))
    side_owner = tuple((a, b - 16) for a, b in side_owner)
    near_owner = tuple((a, b - 16) for a, b in (owner_of(owned + 15), owner_of(owned + 17)))
    own_owner = owner_of(s)
    to_self = (owns_other, jnp.bool_(False))

    def in_copies(t):
        return [
            pltpu.make_async_copy(inv_hbm.at[t], inv.at[t], in_sem.at[t, 0]),
            pltpu.make_async_copy(cpl_hbm.at[t], cpl.at[t], in_sem.at[t, 1]),
            pltpu.make_async_copy(rs_hbm.at[t], rs.at[t], in_sem.at[t, 2]),
        ]

    for t in range(EL):
        for c in in_copies(t):
            c.start()

    barrier = pltpu.get_barrier_semaphore()

    def greet(a, b):
        pl.semaphore_signal(barrier, inc=1, device_id=(a, b), device_id_type=MESH)

    def both(a, b):
        return jnp.logical_and(a, b)

    not_owner = jnp.logical_not(is_owner)
    not_own = jnp.logical_not(owns_own)
    for side in range(2):
        @pl.when(has_side[side])
        def _():
            greet(g, s + shift[side])

            @pl.when(jnp.logical_not(to_self[side]))
            def _():
                greet(*side_owner[side])

        @pl.when(both(is_owner, owned_side[side]))
        def _():
            greet(*near_owner[side])
            for q in range(NB):
                @pl.when(jnp.logical_not(both(owned + shift[side] == s, m == q)))
                def _():
                    greet(block * NB + q, owned + shift[side])

        @pl.when(jnp.logical_not(has_side[side]))
        def _():
            hbuf[side] = jnp.zeros((256, 128), BF16)
            for k in range(SWEEPS - 1):
                xbuf[k, side] = jnp.zeros((EL, FACE, RHS), BF16)
                ebuf[k, side] = jnp.zeros((FACE, RHS), BF16)

        @pl.when(both(is_owner, jnp.logical_not(owned_side[side])))
        def _():
            for k in range(SWEEPS - 1):
                obuf[k, side] = jnp.zeros((NB, FACE, RHS), BF16)
                pbuf[k, side] = jnp.zeros((NB, FACE, RHS), BF16)

    @pl.when(is_owner)
    def _():
        for q in range(NB):
            pl.when(jnp.logical_not(both(owned == s, m == q)))(lambda: greet(block * NB + q, owned))
        for i in range(1, blocks_along):
            greet((g + i * NB) % (blocks_along * NB), s)

    pl.when(not_own)(lambda: greet(*own_owner))

    before = blocks_along - 1
    for j in range(before):
        @pl.when(both(is_owner, j >= block))
        def _():
            chain[:, j * FACE : j * FACE + FACE] = jnp.zeros((FACE, FACE), BF16)
            chain[:, (before + j) * FACE : (before + j) * FACE + FACE] = jnp.zeros((FACE, FACE), BF16)
            for k in range(SWEEPS):
                cin[k, j] = jnp.zeros((FACE, RHS), BF16)

    for t in range(EL):
        for c in in_copies(t):
            c.wait()
        rows = face_groups(inv[t])
        chosen = faces_of(mm_nt(rows, cpl[t]))
        lift_face[t] = left_pair(chosen[:, :FACE])
        side_face[t] = chosen[:, FACE:]
        gain_face[t] = faces_of(mm(rows, rs[t]))

    slots = [order_ref[p] for p in range(EL)]
    trace = None
    pf_mat[...] = jnp.zeros(pf_mat.shape, BF16)
    s_mat[...] = jnp.zeros(s_mat.shape, BF16)
    face_entry = [[None] * EL, [None] * EL]
    for p in range(EL):
        lift = lift_face[slots[p]]
        side = side_face[slots[p]]
        gain = gain_face[slots[p]]
        if p == 0:
            lift_own = lift[:, :FACE].astype(F32) + lift[:, FACE:].astype(F32)
            result = jnp.concatenate([side, gain, lift_own], axis=1)
        else:
            moved = mm_fine(lift, trace)
            result = jnp.concatenate(
                [moved[:, : 128 * p], side, moved[:, 128 * p : 128 * p + 128] + gain, moved[:, 128 * p + 128 :]],
                axis=1,
            )
        wide = 128 * (p + 1)
        for layer in range(2):
            at = 128 + layer * EL * FACE + p * FACE
            part = result[FACE + layer * FACE : 2 * FACE + layer * FACE]
            pf_mat[at : at + FACE, :wide] = part[:, :wide].astype(BF16)
            pf_const[at : at + FACE] = part[:, wide : wide + 128]
            face_entry[layer][p] = part[:, wide + 128 :].astype(BF16)
            ysend[0, layer, p] = part[:, wide : wide + 128].astype(BF16)
        trace = result[:FACE]
        if p < EL - 1:
            s_mat[p * FACE : p * FACE + FACE, :wide] = trace[:, :wide].astype(BF16)
            s_const[p * FACE : p * FACE + FACE] = trace[:, wide : wide + 128]
            se_mat[p * FACE : p * FACE + FACE] = left_pair(trace[:, wide + 128 :])
    own_o = [
        jnp.concatenate([trace[:, 128 * p + 64 * side : 128 * p + 64 * side + 64] for p in range(EL)], axis=1).astype(BF16)
        for side in range(2)
    ]
    for side in range(2):
        fe = face_entry[side]
        hsend[side, :64] = own_o[side][:, :128]
        hsend[side, 64:128] = own_o[side][:, 128:]
        hsend[side, 128:] = jnp.concatenate(
            [jnp.concatenate([fe[0], fe[1]], axis=0), jnp.concatenate([fe[2], fe[3]], axis=0)], axis=1
        )
    msend[:64] = left_pair(trace[:, 640:])
    msend[64:] = trace[:, 512:640].astype(BF16)

    @pl.when(owns_own)
    def _():
        mbuf[m] = msend[...]

    def number(flag):
        return flag.astype(jnp.int32)

    greetings = 2 * (number(has_side[0]) + number(has_side[1])) - number(owns_other) + number(not_own)
    greetings = greetings + number(is_owner) * (
        (NB + 1) * (number(owned_side[0]) + number(owned_side[1]))
        + NB + blocks_along - 1
    ) - number(owns_other) - number(owns_own)
    pl.semaphore_wait(barrier, greetings)

    def remote(src, dst, send, recv, a, b):
        return pltpu.make_async_remote_copy(src, dst, send, recv, device_id=(a, b), device_id_type=MESH)

    def h_copy(side):
        return remote(hsend.at[side], hbuf.at[1 - side], h_s.at[side], h_r.at[1 - side], g, s + shift[side])

    def h_arrival(side):
        return remote(hsend.at[side], hbuf.at[side], h_s.at[side], h_r.at[side], g, s + shift[side])

    def map_copy(who):
        return remote(msend, mbuf.at[who], m_s, m_r.at[who], *own_owner)

    def a_copy(who):
        return remote(asend, abuf.at[who], a_s, a_r.at[who], *own_owner)

    def face_copy(k, side):
        return remote(
            ysend.at[k, side], xbuf.at[k, 1 - side], face_s.at[k, side], face_r.at[k, 1 - side], g, s + shift[side]
        )

    def face_arrival(k, side):
        return remote(ysend.at[k, side], xbuf.at[k, side], face_s.at[k, side], face_r.at[k, side], g, s + shift[side])

    def p_copy(k, side):
        return remote(
            psend.at[k, side], pbuf.at[k, 1 - side, m], p_s.at[k, side], p_r.at[k, 1 - side],
            *side_owner[side],
        )

    def p_local(k, side):
        return pltpu.make_async_copy(psend.at[k, side], pbuf.at[k, 1 - side, m], p_r.at[k, 1 - side])

    def p_start(k, side):
        pl.when(both(has_side[side], jnp.logical_not(to_self[side])))(lambda: p_copy(k, side).start())
        pl.when(both(has_side[side], to_self[side]))(lambda: p_local(k, side).start())

    def p_arrival(k, side):
        return remote(pbuf.at[k, side], pbuf.at[k, side], p_s.at[k, side], p_r.at[k, side], g, s + shift[side])

    def owner_copy(k, side):
        return remote(
            esend.at[k], obuf.at[k, 1 - side], o_s.at[k, side], o_r.at[k, 1 - side], *near_owner[side]
        )

    def owner_arrival(k, side):
        return remote(esend.at[k], obuf.at[k, side], o_s.at[k, side], o_r.at[k, side], g, s + shift[side])

    def entry_copy(k, side, q):
        return remote(
            esend.at[k, q], ebuf.at[k, 1 - side], e_s.at[k, side, q], e_r.at[k, 1 - side],
            block * NB + q, owned + shift[side],
        )

    def entry_local(k, side, q):
        return pltpu.make_async_copy(esend.at[k, q], ebuf.at[k, 1 - side], e_r.at[k, 1 - side])

    def entry_self(side, q):
        return both(owned + shift[side] == s, m == q)

    def entry_arrival(k, side):
        return remote(esend.at[k, 0], ebuf.at[k, side], e_s.at[k, side], e_r.at[k, side], g, s + shift[side])

    def rest_copy(k, ahead):
        return remote(
            csend.at[k], cin.at[k, block], c_s.at[k, ahead - 1], c_r.at[k, block], g + ahead * NB, s
        )

    def rest_arrival(k, j):
        return remote(csend.at[k], cin.at[k, j], c_s.at[k, 0], c_r.at[k, j], g, s)

    def turn_copy(ahead):
        return remote(tsend, tin.at[block], t_s.at[ahead - 1], t_r.at[block], g + ahead * NB, s)

    def turn_arrival(j):
        return remote(tsend, tin.at[j], t_s.at[0], t_r.at[j], g, s)

    def later(ahead):
        return block + ahead < blocks_along

    def send_rest(k):
        csend[k] = local[NB * FACE :].astype(BF16)
        for ahead in range(1, blocks_along):
            pl.when(later(ahead))(lambda: rest_copy(k, ahead).start())

    def form_chain():
        eye = (
            lax.broadcasted_iota(jnp.int32, (FACE, FACE), 0) == lax.broadcasted_iota(jnp.int32, (FACE, FACE), 1)
        ).astype(F32)
        for j in reversed(range(before)):
            @pl.when(j + 1 == block)
            def _():
                running[...] = left_pair(eye)

            if j + 1 < before:
                @pl.when(j + 1 < block)
                def _():
                    turn_arrival(j + 1).wait_recv()
                    turn = tin[j + 1, :, :FACE].astype(F32) + tin[j + 1, :, FACE:].astype(F32)
                    running[...] = left_pair(mm_fine(running[...], turn))

            @pl.when(j < block)
            def _():
                chain[:, j * FACE : j * FACE + FACE] = running[:, :FACE]
                chain[:, (before + j) * FACE : (before + j) * FACE + FACE] = running[:, FACE:]

        pl.when(has_up)(lambda: turn_arrival(0).wait_recv())

    def last_copy(q):
        return remote(esend.at[SWEEPS - 1, q], efin, fin_s.at[q], fin_r, block * NB + q, owned)

    pl.when(not_own)(lambda: map_copy(m).start())
    for side in range(2):
        pl.when(has_side[side])(lambda: h_copy(side).start())
    for side in range(2):
        pl.when(has_side[side])(lambda: face_copy(0, side).start())

    for t in range(EL):
        maps = mm_nt(inv[t], cpl[t])
        lift_full[t] = left_pair(maps[:, :FACE])
        side_full[t] = maps[:, FACE:].astype(BF16)
        gain_full[t] = mm(inv[t], rs[t])

    def owner_finish(k, final):
        for j in range(before):
            pl.when(j < block)(lambda: rest_arrival(k, j).wait_recv())
        rests = jnp.concatenate([cin[k, j] for j in range(before)], axis=0)
        carried = twice(mm(chain[...], twice(rests)).astype(BF16))
        entries = (local[: NB * FACE] + mm(d_all[: NB * FACE], carried)).astype(BF16)
        for q in range(NB):
            esend[k, q] = entries[q * FACE : q * FACE + FACE]
        if final:
            for q in range(NB):
                pl.when(jnp.logical_not(both(owned == s, m == q)))(lambda: last_copy(q).start())

            @pl.when(owns_own)
            def _():
                efin[...] = esend[k, m]
        else:
            for side in range(2):
                @pl.when(owned_side[side])
                def _():
                    for q in range(NB):
                        pl.when(jnp.logical_not(entry_self(side, q)))(lambda: entry_copy(k, side, q).start())
                        pl.when(entry_self(side, q))(lambda: entry_local(k, side, q).start())
            for side in range(2):
                pl.when(owned_side[side])(lambda: owner_copy(k, side).start())

    @pl.when(is_owner)
    def _():
        for q in range(NB):
            pl.when(jnp.logical_not(both(owned == s, m == q)))(lambda: map_copy(q).wait_recv())
        eye = (
            lax.broadcasted_iota(jnp.int32, (FACE, FACE), 0) == lax.broadcasted_iota(jnp.int32, (FACE, FACE), 1)
        ).astype(F32)
        none = jnp.zeros((FACE, FACE), F32)
        state = jnp.concatenate([none] * NB + [eye], axis=1)
        for q in range(NB + 1):
            m_all[q * FACE : q * FACE + FACE] = left_pair(state[:, : NB * FACE])
            d_all[q * FACE : q * FACE + FACE] = left_pair(state[:, NB * FACE :])
            if q < NB:
                state = mm_fine(mbuf[q, :64], state) + jnp.concatenate(
                    [eye if r == q else none for r in range(NB)] + [none], axis=1
                )
        tsend[...] = d_all[NB * FACE :]
        for ahead in range(1, blocks_along):
            pl.when(later(ahead))(lambda: turn_copy(ahead).start())
        starts = jnp.concatenate([mbuf[q, 64:] for q in range(NB)], axis=0)
        local[...] = mm(m_all[...], twice(starts))
        send_rest(0)
        pl.when(jnp.logical_not(has_up))(lambda: owner_finish(0, False))

    for side in range(2):
        pl.when(has_side[side])(lambda: h_arrival(side).wait_recv())
    from_o = [jnp.concatenate([hbuf[side, :64], hbuf[side, 64:128]], axis=1) for side in range(2)]
    from_fe = [jnp.concatenate([hbuf[side, 128:, :64], hbuf[side, 128:, 64:]], axis=0) for side in range(2)]
    for side in range(2):
        at = 128 + side * EL * FACE
        pf_const[64 * side : 64 * side + 64] = mm(from_o[side], pf_const[at : at + 256].astype(BF16))
        psend[0, side] = pf_const[64 * side : 64 * side + 64].astype(BF16)
        p_start(0, side)
    asend[...] = jnp.concatenate([mm(own_o[side], from_fe[side]) for side in range(2)], axis=1).astype(BF16)
    pl.when(not_own)(lambda: a_copy(m).start())

    @pl.when(owns_own)
    def _():
        abuf[m] = asend[...]

    blank = jnp.zeros((FACE, FACE), BF16)
    for side in range(2):
        at = 128 + side * EL * FACE
        pf_mat[64 * side : 64 * side + 64] = mm(from_o[side], pf_mat[at : at + 256]).astype(BF16)
        for p in range(EL):
            part = from_fe[side][p * FACE : p * FACE + FACE]
            row = 128 * p + 64 * side
            fe_next[row : row + FACE] = jnp.concatenate([part, blank] if side == 0 else [blank, part], axis=1)

    @pl.when(is_owner)
    def _():
        @pl.when(has_up)
        def _():
            form_chain()
            owner_finish(0, False)

        for q in range(NB):
            pl.when(jnp.logical_not(both(owned == s, m == q)))(lambda: a_copy(q).wait_recv())

    def owner_gather(k):
        for side in range(2):
            @pl.when(owned_side[side])
            def _():
                p_arrival(k, side).wait_recv()
                owner_arrival(k, side).wait_recv()
        offsets = []
        for q in range(NB):
            known = mbuf[q, 64:].astype(F32) + pbuf[k, 0, q].astype(F32) + pbuf[k, 1, q].astype(F32)
            coming = jnp.concatenate([obuf[k, 0, q], obuf[k, 1, q]], axis=0)
            offsets.append((known + mm(abuf[q], coming)).astype(BF16))
        local[...] = mm(m_all[...], twice(jnp.concatenate(offsets, axis=0)))
        send_rest(k + 1)

    def member_gather(k):
        for side in range(2):
            @pl.when(has_side[side])
            def _():
                entry_arrival(k, side).wait_recv()
                face_arrival(k, side).wait_recv()
        early = jnp.concatenate([xbuf[k, side, p] for p in range(EL) for side in range(2)], axis=0)
        entries = jnp.concatenate([ebuf[k, 0], ebuf[k, 1]], axis=0)
        now = (early.astype(F32) + mm(fe_next[...], entries)).astype(BF16)
        for p in range(EL):
            xs[p] = now[128 * p : 128 * p + 128]
        return now

    @pl.loop(0, SWEEPS - 2)
    def _(k):
        now = member_gather(k)
        ahead = (mm(pf_mat[:128], now) + pf_const[:128]).astype(BF16)
        for side in range(2):
            psend[k + 1, side] = ahead[64 * side : 64 * side + 64]
            p_start(k + 1, side)
        for side in range(2):
            at = 128 + side * EL * FACE
            ahead = (mm(pf_mat[at : at + 256], now) + pf_const[at : at + 256]).astype(BF16)
            for p in range(EL):
                ysend[k + 1, side, p] = ahead[p * FACE : p * FACE + FACE]
            pl.when(has_side[side])(lambda: face_copy(k + 1, side).start())

        @pl.when(is_owner)
        def _():
            owner_gather(k)
            owner_finish(k + 1, False)

    last = SWEEPS - 1

    @pl.when(is_owner)
    def _():
        owner_gather(last - 1)
        owner_finish(last, True)

    now = member_gather(last - 1)
    places = []
    for t in range(EL):
        place = jnp.int32(0)
        for p in range(1, EL):
            place = jnp.where(slots[p] == t, p, place)
        places.append(place)
    traces = mm(s_mat[...], now) + s_const[...]
    for t in range(EL):
        pre_out[t] = gain_full[t] + mm(side_full[t], xs[places[t]])
    pl.when(not_own)(lambda: last_copy(m).wait_recv())
    entry = efin[...]
    traces = (traces + mm(se_mat[...], twice(entry))).astype(BF16)
    inflow[0] = entry
    for p in range(1, EL):
        inflow[p] = traces[(p - 1) * FACE : p * FACE]

    def out_copy(t):
        return pltpu.make_async_copy(out_v.at[t], out_hbm.at[t], out_sem.at[t])

    for t in range(EL):
        out_v[t] = (pre_out[t] + mm(lift_full[t], twice(inflow[places[t]]))).astype(BF16)
        out_copy(t).start()

    @pl.when(not_own)
    def _():
        map_copy(m).wait_send()
        a_copy(m).wait_send()

    for side in range(2):
        pl.when(has_side[side])(lambda: h_copy(side).wait_send())

    @pl.loop(0, SWEEPS - 1)
    def _(k):
        for side in range(2):
            pl.when(has_side[side])(lambda: face_copy(k, side).wait_send())
            pl.when(both(has_side[side], jnp.logical_not(to_self[side])))(lambda: p_copy(k, side).wait_send())

            @pl.when(both(is_owner, owned_side[side]))
            def _():
                owner_copy(k, side).wait_send()
                for q in range(NB):
                    pl.when(jnp.logical_not(entry_self(side, q)))(lambda: entry_copy(k, side, q).wait_send())

    @pl.when(is_owner)
    def _():
        for ahead in range(1, blocks_along):
            @pl.when(later(ahead))
            def _():
                turn_copy(ahead).wait_send()

                @pl.loop(0, SWEEPS)
                def _(k):
                    rest_copy(k, ahead).wait_send()

        for q in range(NB):
            pl.when(jnp.logical_not(both(owned == s, m == q)))(lambda: last_copy(q).wait_send())

    for t in range(EL):
        out_copy(t).wait()


def shards(blocks_along, spans, right_sides, inverse, coupling, sweep_order):
    vmem = pltpu.VMEM
    dma = pltpu.SemaphoreType.DMA
    hbm = pl.BlockSpec(memory_space=pltpu.HBM)
    trips = SWEEPS - 1
    before = blocks_along - 1
    placed = pl.pallas_call(
        lambda *refs: kernel(blocks_along, spans, *refs),
        name="sweeps",
        out_shape=jax.ShapeDtypeStruct((EL, NODES, RHS), BF16),
        in_specs=[pl.BlockSpec(memory_space=pltpu.SMEM), hbm, hbm, hbm],
        out_specs=hbm,
        scratch_shapes=[
            vmem((EL, NODES, RHS), BF16),
            vmem((EL, NODES, NODES), BF16),
            vmem((EL, 3 * FACE, NODES), BF16),
            vmem((EL, NODES, RHS), BF16),
            vmem((EL, NODES, 2 * FACE), BF16),
            vmem((EL, NODES, 2 * FACE), BF16),
            vmem((EL, NODES, RHS), F32),
            vmem((EL, 3 * FACE, 2 * FACE), BF16),
            vmem((EL, 3 * FACE, 2 * FACE), F32),
            vmem((EL, 3 * FACE, RHS), F32),
            vmem((640, 512), BF16),
            vmem((640, RHS), F32),
            vmem((512, 128), BF16),
            vmem((3 * FACE, 512), BF16),
            vmem((3 * FACE, 2 * FACE), BF16),
            vmem((3 * FACE, RHS), F32),
            vmem(((NB + 1) * FACE, 2 * NB * FACE), BF16),
            vmem(((NB + 1) * FACE, 2 * FACE), BF16),
            vmem(((NB + 1) * FACE, RHS), F32),
            vmem((EL, FACE, RHS), BF16),
            vmem((EL, 2 * FACE, RHS), BF16),
            vmem((EL, NODES, RHS), F32),
            vmem((2, 256, 128), BF16),
            vmem((2, 256, 128), BF16),
            vmem((128, 128), BF16),
            vmem((FACE, 128), BF16),
            vmem((NB, 128, 128), BF16),
            vmem((NB, FACE, 128), BF16),
            vmem((trips, 2, EL, FACE, RHS), BF16),
            vmem((trips, 2, EL, FACE, RHS), BF16),
            vmem((trips, 2, FACE, RHS), BF16),
            vmem((trips, 2, NB, FACE, RHS), BF16),
            vmem((SWEEPS, NB, FACE, RHS), BF16),
            vmem((trips, 2, NB, FACE, RHS), BF16),
            vmem((trips, 2, FACE, RHS), BF16),
            vmem((SWEEPS, before, FACE, RHS), BF16),
            vmem((SWEEPS, FACE, RHS), BF16),
            vmem((before, FACE, 128), BF16),
            vmem((FACE, 128), BF16),
            vmem((FACE, 2 * before * FACE), BF16),
            vmem((FACE, 128), BF16),
            vmem((FACE, RHS), BF16),
            dma((EL, 3)),
            dma((EL,)),
            dma((2,)),
            dma((2,)),
            dma,
            dma((NB,)),
            dma,
            dma((NB,)),
            dma((trips, 2)),
            dma((trips, 2)),
            dma((trips, 2, NB)),
            dma((trips, 2)),
            dma((trips, 2)),
            dma((trips, 2)),
            dma((trips, 2)),
            dma((trips, 2)),
            dma((SWEEPS, before)),
            dma((SWEEPS, before)),
            dma((before,)),
            dma((before,)),
            dma((NB,)),
            dma,
        ],
        compiler_params=pltpu.CompilerParams(
            collective_id=0, has_side_effects=True, vmem_limit_bytes=58 * 2**20
        ),
    )(
        sweep_order[0, 0],
        right_sides[0, 0],
        inverse[0, 0],
        coupling[0, 0].reshape(EL, 3 * FACE, NODES),
    )
    return placed[None, None]


def solution(mesh):
    blocks_along = mesh.shape["stream"] // NB
    spans = mesh.shape["span"]
    in_specs = (
        P("stream", "span", None, None, None),
        P("stream", "span", None, None, None),
        P("stream", "span", None, None, None, None),
        P("stream", "span", None),
    )
    out_specs = P("stream", "span", None, None, None)

    def run(right_sides, inverse, coupling, sweep_order):
        return shards(blocks_along, spans, right_sides, inverse, coupling, sweep_order)

    return jax.shard_map(run, mesh=mesh, in_specs=in_specs, out_specs=out_specs, check_vma=False)
```
